256 devices in a mesh: sy: 16 (over z_lo, y, core), sx: 4 (over x), cls: 4 (over z_hi).
Axes of the slice: x: 4, y: 4, z: 8 (z_hi: 4, z_lo: 2; z = z_hi * 2 + z_lo), core: 2. Of those that a mesh axis runs over, the one named last changes fastest.
Arguments:
- adjoint_final: float32 [64, 1024, 1536], P('cls', 'sy', 'sx'), may hold values from -6 to 6
- stored_states: bfloat16 [2, 64, 1024, 1536], P(None, 'cls', 'sy', 'sx'), may hold values from 0.049804688 to 2
- habitat: int32 [1024, 1536], P('sy', 'sx'), may hold values from 0 to 7
- growth: float32 [64, 64], replicated, may hold values from -0.75 to 0.75
- survival: float32 [8, 64], replicated, may hold values from 0.3 to 1
- fecundity: float32 [8, 64], replicated, may hold values from 0.1 to 3
- recruit: float32 [64], replicated, may hold values from 0 to 0.25
- disp_rows: float32 [15], replicated, may hold values from 0.02 to 0.2
- disp_cols: float32 [15], replicated, may hold values from 0.02 to 0.2
Outputs:
- adjoint_start: float32 [64, 1024, 1536], P('cls', 'sy', 'sx')
- survival_sens: float32 [2, 64, 1024, 1536], P(None, 'cls', 'sy', 'sx')
The draws below stay inside these ranges and needn't reach their ends.
All inputs are finite; a program needn't handle non-finite values.
Results may differ from the reference program's by a relative error of at most 0.0003.
Values sent between devices are 32-bit elements; how exact they have to be, the bound alone decides.
A program may use at most 64 MiB of HBM per device.

```python
import math
import jax
import jax.numpy as jnp
from jax import lax

NC = 64
NH = 8
REACH = 7
YEARS = 2
TAPS = 15
NY = 1024
NX = 1536


def set_ends(drawn, stream_key, low, high):
    longest = drawn.shape.index(max(drawn.shape))
    spots = []
    for shift in (0, 1):
        where = [jax.random.randint(jax.random.fold_in(stream_key, axis), (), 0, length) for axis, length in enumerate(drawn.shape)]
        where[longest] = (where[longest] + shift) % drawn.shape[longest]
        spots.append(tuple(where))
    return drawn.at[spots[0]].set(low).at[spots[1]].set(high)


def steps_of(stream_key, extent, pieces, smallest, top_value):
    def one(axis_at, blocks):
        steps = jax.random.uniform(jax.random.fold_in(jax.random.fold_in(stream_key, 6), axis_at), (blocks,), jnp.float32, smallest / len(pieces), top_value / len(pieces))
        return jnp.repeat(jnp.exp(steps), extent[axis_at] // blocks).reshape((-1,) + (1,) * (len(extent) - axis_at - 1))

    loudness = one(*pieces[0])
    for cut in pieces[1:]:
        loudness = loudness * one(*cut)
    return loudness


def centred(stream_key, dims, deviation, bound, cuts=(), dtype=jnp.bfloat16):
    loudness = steps_of(stream_key, dims, cuts, -0.22, 0.18) if cuts else 1.0
    values = jax.random.normal(stream_key, dims, jnp.float32) * deviation * loudness
    return jnp.minimum(jnp.maximum(values, -bound), bound).astype(dtype)


def setup_inputs(seed: int = 0) -> dict:
    keys = jax.random.split(jax.random.key(seed), 10)
    adjoint_final = centred(keys[0], (NC, NY, NX), 1.0, 6.0, ((0, 4), (1, 16), (2, 4)), jnp.float32)
    stored_states = jnp.clip(jnp.exp(math.log(2.0) - 3.6927934 * jax.random.uniform(keys[1], (YEARS, NC, NY, NX), jnp.float32) ** steps_of(keys[1], (YEARS, NC, NY, NX), ((1, 4), (2, 16), (3, 4)), -0.2, 0.2)), 0.049804688, 2.0).astype(jnp.bfloat16)
    habitat = set_ends(jax.random.randint(keys[2], (NY, NX), 0, NH), jax.random.fold_in(keys[2], 1), 0, NH - 1).astype(jnp.int32)
    growth = centred(keys[3], (NC, NC), NC ** -0.5, 0.75, (), jnp.float32)
    survival = jnp.clip(jax.random.uniform(keys[4], (NH, NC), jnp.float32, 0.3, 1.0), 0.3, 1.0)
    fecundity = jnp.clip(jnp.exp(jax.random.uniform(keys[5], (NH, NC), jnp.float32, math.log(0.1), math.log(3.0))), 0.1, 3.0)
    recruit = jnp.clip(jax.random.uniform(keys[6], (NC,), jnp.float32, 0.0, 0.25), 0.0, 0.25)
    disp_rows = jnp.clip(jnp.exp(jax.random.uniform(keys[7], (TAPS,), jnp.float32, math.log(0.02), math.log(0.2))), 0.02, 0.2)
    disp_cols = jnp.clip(jnp.exp(jax.random.uniform(keys[8], (TAPS,), jnp.float32, math.log(0.02), math.log(0.2))), 0.02, 0.2)
    return dict(adjoint_final=adjoint_final, stored_states=stored_states, habitat=habitat, growth=growth, survival=survival, fecundity=fecundity, recruit=recruit, disp_rows=disp_rows, disp_cols=disp_cols)


def disperse(seed_value, disp_rows, disp_cols):
    padded = jnp.pad(seed_value, REACH)
    across = disp_rows[0] * padded[0:NY, :]
    for offset in range(1, TAPS):
        across = across + disp_rows[offset] * padded[offset:offset + NY, :]
    result = disp_cols[0] * across[:, 0:NX]
    for offset in range(1, TAPS):
        result = result + disp_cols[offset] * across[:, offset:offset + NX]
    return result


def reference(adjoint_final, stored_states, habitat, growth, survival, fecundity, recruit, disp_rows, disp_cols):
    rate_surv = jnp.transpose(survival[habitat], (2, 0, 1))
    rate_fec = jnp.transpose(fecundity[habitat], (2, 0, 1))
    adjoint = adjoint_final
    sensitivity = [None] * YEARS
    for period in range(YEARS - 1, -1, -1):
        carried = jnp.einsum('ij,iyx->jyx', growth, adjoint, precision=lax.Precision.HIGHEST)
        seed_value = jnp.einsum('i,iyx->yx', recruit, adjoint, precision=lax.Precision.HIGHEST)
        spread = disperse(seed_value, disp_rows, disp_cols)
        sensitivity[period] = stored_states[period].astype(jnp.float32) * carried
        adjoint = rate_surv * carried + rate_fec * spread[None]
    return adjoint, jnp.stack(sensitivity)
```

```python
import functools

import jax
import jax.numpy as jnp
from jax import lax
from jax.experimental import pallas as pl
from jax.experimental.pallas import tpu as pltpu
from jax.sharding import PartitionSpec as P

MESH = pl.DeviceIdType.MESH
F32 = jnp.float32
BF16 = jnp.bfloat16
HIGH = lax.Precision.HIGHEST

SUB = 8
NEXT, OWN, REC, PREV, FAR = 0, 128, 256, 272, 400
ROWS_W = 528
HALO = 16
SIDE = 128


def dot_t(a, b):
    return lax.dot_general(a, b, (((1,), (1,)), ((), ())), precision=HIGH, preferred_element_type=F32)


def dot_h(a, b):
    return jnp.dot(a, b, precision=HIGH, preferred_element_type=F32)


def iota(shape, dim):
    return lax.broadcasted_iota(jnp.int32, shape, dim)


def split(x):
    hi = x.astype(BF16)
    return hi, (x - hi.astype(F32)).astype(BF16)


def kernel(
    a_hbm, st_hbm, hab, growth, surv, fec, rec, wr, wc,
    adj_out, sens_out,
    own, st_raw, st, gath, wh, wl, xh, xl, rs_all, tabs, c1_all, d_all, c1_snd, d_snd, planes, mid, seed0, sp1, sp0,
    lsem, send, recv,
):
    ncls = 4
    p = lax.axis_index("cls")
    sy, sx = lax.axis_index("sy"), lax.axis_index("sx")
    nsy, nsx = lax.axis_size("sy"), lax.axis_size("sx")
    right, left = lax.rem(p + 1, ncls), lax.rem(p + ncls - 1, ncls)
    below, above = lax.rem(sy + 1, nsy), lax.rem(sy + nsy - 1, nsy)
    east, west = lax.rem(sx + 1, nsx), lax.rem(sx + nsx - 1, nsx)
    classes, rows, cols = own.shape
    quarter = rows // ncls
    inner = pl.ds(SIDE, cols)

    load_a = pltpu.make_async_copy(a_hbm, own, lsem.at[0])
    load_s = pltpu.make_async_copy(st_hbm, st_raw, lsem.at[1])
    load_a.start()
    load_s.start()

    barrier = pltpu.get_barrier_semaphore()
    for where in ({"cls": left}, {"cls": right}, {"sy": above}, {"sy": below}, {"sx": west}, {"sx": east}):
        pl.semaphore_signal(barrier, inc=1, device_id=where, device_id_type=MESH)

    def q_row(ahead, s):
        return pl.multiple_of(lax.rem(p + ahead, ncls) * quarter + s * SUB, SUB)

    def remote(src, dst, k, where):
        return pltpu.make_async_remote_copy(
            src_ref=src, dst_ref=dst, send_sem=send.at[k], recv_sem=recv.at[k], device_id=where, device_id_type=MESH
        )

    to_right, to_left = {"cls": right}, {"cls": left}
    piece = lambda ref, row: ref.at[:, pl.ds(row, SUB), :]
    far_r = [remote(piece(own, q_row(1, s)), gath.at[0, s, 1], 0 + s, to_right) for s in range(2)]
    far_l = [remote(piece(own, q_row(2, s)), gath.at[1, s, 0], 2 + s, to_left) for s in range(2)]
    near_r = [remote(piece(own, q_row(0, s)), gath.at[1, s, 1], 4 + s, to_right) for s in range(2)]
    near_l = [remote(piece(own, q_row(3, s)), gath.at[0, s, 0], 6 + s, to_left) for s in range(2)]
    fwd_r = [remote(gath.at[0, s, 1], gath.at[1, s, 2], 8 + s, to_right) for s in range(2)]
    fwd_l = [remote(gath.at[1, s, 0], gath.at[0, s, 2], 10 + s, to_left) for s in range(2)]
    ret_c = [
        [remote(c1_snd.at[0, s], piece(c1_all, q_row(0, s)), 12 + s, to_left) for s in range(2)],
        [remote(c1_snd.at[1, s], piece(c1_all, q_row(3, s)), 14 + s, to_right) for s in range(2)],
    ]
    ret_d = [
        [remote(d_snd.at[0, s], piece(d_all, q_row(0, s)), 16 + s, to_left) for s in range(2)],
        [remote(d_snd.at[1, s], piece(d_all, q_row(3, s)), 18 + s, to_right) for s in range(2)],
    ]

    def seed_part(ahead):
        return planes.at[pl.ds(0, 2), pl.ds(pl.multiple_of(HALO + q_row(ahead, 0), SUB), quarter), inner]

    seed_l = remote(seed_part(0), seed_part(0), 20, to_left)
    seed_r = remote(seed_part(3), seed_part(3), 21, to_right)
    halo_d = remote(
        planes.at[:, pl.ds(rows, HALO), inner], planes.at[:, pl.ds(0, HALO), inner], 22, {"sy": below}
    )
    halo_u = remote(
        planes.at[:, pl.ds(HALO, HALO), inner], planes.at[:, pl.ds(HALO + rows, HALO), inner], 23, {"sy": above}
    )
    halo_e = remote(planes.at[:, :, pl.ds(cols, SIDE)], planes.at[:, :, pl.ds(0, SIDE)], 24, {"sx": east})
    halo_w = remote(
        planes.at[:, :, pl.ds(SIDE, SIDE)], planes.at[:, :, pl.ds(SIDE + cols, SIDE)], 25, {"sx": west}
    )

    pl.semaphore_wait(barrier, 6)
    load_a.wait()
    for s in range(2):
        far_r[s].start()
        far_l[s].start()
    for s in range(2):
        near_r[s].start()
        near_l[s].start()

    def place_of(rel):
        return ((p + rel) & (ncls - 1)) * classes

    r = iota((ROWS_W, 64), 0)
    base = jnp.where(r < OWN, place_of(1), jnp.where(r < REC, place_of(0), jnp.where(r < FAR, place_of(3), place_of(2))))
    off = jnp.where(r < REC, r & 127, (r - PREV) & 127) >> 3
    is_rec = (r >= REC) & (r < PREV)
    pick = jnp.where((base + off == iota((ROWS_W, 64), 1)) & ~is_rec, 1.0, 0.0).astype(F32)
    g = growth[...]
    by_source = dot_t(pick, g) + jnp.where(is_rec, rec[...], 0.0)
    c = iota((512, 64), 0)
    place_c = jnp.where(c < 128, place_of(1), jnp.where(c < 256, place_of(0), jnp.where(c < 384, place_of(3), place_of(2))))
    pick_c = jnp.where(place_c + ((c & 127) >> 3) == iota((512, 64), 1), 1.0, 0.0).astype(F32)
    full = dot_t(by_source, pick_c)
    full = jnp.where((iota(full.shape, 0) & 7) == (iota(full.shape, 1) & 7), full, 0.0)
    w_hi, w_lo = split(full)
    wh[...] = w_hi
    wl[...] = w_lo

    level = jnp.where((iota((64, 8), 0) >> 3) == iota((64, 8), 1), 1.0, 0.0).astype(F32)

    def expand(table):
        wide = dot_t(table, level)
        return jnp.where((iota(wide.shape, 0) & 7) == (iota(wide.shape, 1) & 7), wide, 0.0)

    s_tab, f_tab = surv[...], fec[...]
    pick_own = pick[OWN:REC]
    k_surv = expand(dot_t(pick, s_tab))
    k_surv = jnp.concatenate([k_surv[:REC], k_surv[PREV:]], axis=0)
    gf_tab = dot_h(f_tab, g)
    rf_one = jnp.broadcast_to(rec[...], (8, 64))
    k_own = jnp.concatenate(
        [
            expand(dot_t(pick_own, s_tab)),
            expand(dot_t(pick_own, f_tab)),
            expand(dot_t(pick_own, gf_tab)),
            expand(dot_t(rf_one, f_tab)),
        ],
        axis=0,
    )

    def indicator(row):
        h = hab[pl.ds(row, SUB), :]
        return jnp.concatenate([jnp.where(h == k, 1.0, 0.0).astype(F32) for k in range(8)], axis=0)

    for kind in range(2):
        for s in range(2):
            rs_all[kind, s] = dot_h(k_surv, indicator(q_row(3 * kind, s)))

    def own_tables(t, carry):
        row = pl.multiple_of(t * SUB, SUB)
        res = dot_h(k_own, indicator(row))
        tabs[t] = res[:384]
        planes[2, pl.ds(pl.multiple_of(HALO + row, SUB), SUB), inner] = res[384:]
        return carry

    lax.fori_loop(0, rows // SUB, own_tables, 0)

    load_s.wait()

    def widen(k, carry):
        st[0, k] = st_raw[0, k].astype(F32)
        st[1, k] = st_raw[1, k].astype(F32)
        return carry

    lax.fori_loop(0, classes, widen, 0)

    for s in range(2):
        far_r[s].wait_recv()
        fwd_r[s].start()
        far_l[s].wait_recv()
        fwd_l[s].start()

    def flat(x):
        return x.reshape(classes * SUB, cols)

    def product(lo, hi):
        a_hi, a_lo = xh[...], xl[...]
        w1, w2 = wh[lo:hi], wl[lo:hi]
        return (
            jnp.dot(w1, a_hi, preferred_element_type=F32)
            + jnp.dot(w1, a_lo, preferred_element_type=F32)
            + jnp.dot(w2, a_hi, preferred_element_type=F32)
        )

    def process(kind, s):
        row = q_row(3 * kind, s)
        prow = pl.multiple_of(HALO + row, SUB)
        blocks = (gath[kind, s, 0], own[:, pl.ds(row, SUB), :], gath[kind, s, 1], gath[kind, s, 2])
        for k, block in enumerate(blocks):
            xh[k * 128 : (k + 1) * 128], xl[k * 128 : (k + 1) * 128] = split(flat(block))
        res = product(0, ROWS_W)
        there = (res[PREV:FAR], res[NEXT:OWN])[kind]
        c1_snd[kind, s] = there.reshape(classes, SUB, cols)
        c1_all[:, pl.ds(row, SUB), :] = res[OWN:REC].reshape(classes, SUB, cols)
        planes[0, pl.ds(prow, SUB), inner] = res[REC : REC + SUB]
        for k, start in enumerate((NEXT, OWN, PREV, FAR)):
            xh[k * 128 : (k + 1) * 128], xl[k * 128 : (k + 1) * 128] = split(
                res[start : start + 128] * rs_all[kind, s, k * 128 : (k + 1) * 128]
            )
        if kind == 0:
            res = product(OWN, FAR)
            mine, seeds, there = res[:128], res[128:136], res[144:272]
        else:
            res = product(NEXT, PREV)
            there, mine, seeds = res[:128], res[128:256], res[256:264]
        d_snd[kind, s] = there.reshape(classes, SUB, cols)
        d_all[:, pl.ds(row, SUB), :] = mine.reshape(classes, SUB, cols)
        planes[1, pl.ds(prow, SUB), inner] = seeds

    def arrive(s):
        near_l[s].wait_recv()
        fwd_l[s].wait_recv()
        near_r[s].wait_recv()
        fwd_r[s].wait_recv()

    arrive(0)
    for kind in range(2):
        process(kind, 0)
        ret_c[kind][0].start()
    arrive(1)
    for kind in range(2):
        process(kind, 1)
    seed_l.start()
    seed_r.start()
    for kind in range(2):
        ret_d[kind][0].start()
    for kind in range(2):
        ret_c[kind][1].start()
    for kind in range(2):
        ret_d[kind][1].start()

    seed_l.wait_recv()
    seed_r.wait_recv()
    halo_d.start()
    halo_u.start()
    halo_d.wait_recv()
    halo_u.wait_recv()
    halo_e.start()
    halo_w.start()
    halo_e.wait_recv()
    halo_w.wait_recv()
    halo_d.wait_send()
    halo_u.wait_send()
    halo_e.wait_send()
    halo_w.wait_send()

    def inside(shape, first):
        y = iota(shape, 0) + (first - HALO) + sy * rows
        x = iota(shape, 1) - SIDE + sx * cols
        return (y >= 0) & (y < nsy * rows) & (x >= 0) & (x < nsx * cols)

    wide = cols + 2 * SIDE
    taps = wr.shape[0]
    reach = taps // 2

    def along_rows(load, row):
        total = wr[0] * load(row - reach)
        for k in range(1, taps):
            total = total + wr[k] * load(row - reach + k)
        return total

    def along_cols(x):
        total = wc[reach] * x
        for k in range(taps):
            if k != reach:
                total = total + wc[k] * pltpu.roll(x, (reach - k) % wide, axis=1)
        return total

    n_pad = rows + 2 * HALO

    for t in range(n_pad // SUB):
        at = pl.ds(t * SUB, SUB)
        mid[at, :] = jnp.where(inside((SUB, wide), t * SUB), planes[0, at, :], 0.0)
    for t in range(1, n_pad // SUB - 1):
        at = pl.ds(t * SUB, SUB)
        spread = along_cols(along_rows(lambda first: mid[pl.ds(first, SUB), :], t * SUB))
        if 2 <= t < 2 + rows // SUB:
            sp1[pl.ds((t - 2) * SUB, SUB), :] = spread[:, SIDE : SIDE + cols]
        seed0[at, :] = jnp.where(
            inside((SUB, wide), t * SUB), planes[1, at, :] + planes[2, at, :] * spread, 0.0
        )
    for t in range(2, 2 + rows // SUB):
        spread = along_cols(along_rows(lambda first: seed0[pl.ds(first, SUB), :], t * SUB))
        sp0[pl.ds((t - 2) * SUB, SUB), :] = spread[:, SIDE : SIDE + cols]

    def finish_c(row):
        at = pl.ds(row, SUB)
        sens_out[1, :, at, :] = st[1, :, at, :] * c1_all[:, at, :]

    def finish_d(row):
        at = pl.ds(row, SUB)
        t = row // SUB
        cube = lambda k: tabs[t, k * 128 : (k + 1) * 128].reshape(classes, SUB, cols)
        carried = d_all[:, at, :] + cube(2) * sp1[at, :][None]
        sens_out[0, :, at, :] = st[0, :, at, :] * carried
        adj_out[:, at, :] = cube(0) * carried + cube(1) * sp0[at, :][None]

    for kind in range(2):
        for s in range(2):
            finish_c(q_row(3 * kind, s))
            finish_d(q_row(3 * kind, s))
    for s in range(2):
        for kind in range(2):
            ret_c[kind][s].wait_recv()
            finish_c(q_row(1 + kind, s))
        for kind in range(2):
            ret_d[kind][s].wait_recv()
            finish_d(q_row(1 + kind, s))
    for group in (far_r, far_l, near_r, near_l, fwd_r, fwd_l, *ret_c, *ret_d, [seed_l, seed_r]):
        for copy in group:
            copy.wait_send()


def per_device(
    adjoint_final, stored_states, habitat, growth, survival, fecundity, recruit, disp_rows, disp_cols
):
    years, classes, rows, cols = stored_states.shape
    wide = cols + 2 * SIDE
    block = (classes, rows, cols)
    vmem = pl.BlockSpec(memory_space=pltpu.VMEM)
    smem = pl.BlockSpec(memory_space=pltpu.SMEM)
    hbm = pl.BlockSpec(memory_space=pl.ANY)
    packs = (2, 2, classes, SUB, cols)
    return pl.pallas_call(
        kernel,
        out_shape=(jax.ShapeDtypeStruct(block, F32), jax.ShapeDtypeStruct((years,) + block, F32)),
        in_specs=[hbm, hbm, vmem, vmem, vmem, vmem, vmem, smem, smem],
        out_specs=(vmem, vmem),
        scratch_shapes=[
            pltpu.VMEM(block, F32),
            pltpu.VMEM((years,) + block, BF16),
            pltpu.VMEM((years,) + block, F32),
            pltpu.VMEM((2, 2, 3, classes, SUB, cols), F32),
            pltpu.VMEM((ROWS_W, 512), BF16),
            pltpu.VMEM((ROWS_W, 512), BF16),
            pltpu.VMEM((512, cols), BF16),
            pltpu.VMEM((512, cols), BF16),
            pltpu.VMEM((2, 2, 512, cols), F32),
            pltpu.VMEM((rows // SUB, 384, cols), F32),
            pltpu.VMEM(block, F32),
            pltpu.VMEM(block, F32),
            pltpu.VMEM(packs, F32),
            pltpu.VMEM(packs, F32),
            pltpu.VMEM((3, rows + 2 * HALO, wide), F32),
            pltpu.VMEM((rows + 2 * HALO, wide), F32),
            pltpu.VMEM((rows + 2 * HALO, wide), F32),
            pltpu.VMEM((rows, cols), F32),
            pltpu.VMEM((rows, cols), F32),
            pltpu.SemaphoreType.DMA((2,)),
            pltpu.SemaphoreType.DMA((26,)),
            pltpu.SemaphoreType.DMA((26,)),
        ],
        compiler_params=pltpu.CompilerParams(
            collective_id=0, has_side_effects=True, vmem_limit_bytes=50 << 20
        ),
        cost_estimate=pl.CostEstimate(flops=4 * 10**9, bytes_accessed=8 * 10**6, transcendentals=0),
    )(
        adjoint_final, stored_states, habitat, growth, survival, fecundity, recruit.reshape(1, -1),
        disp_rows, disp_cols,
    )


def solution(mesh):
    return jax.shard_map(
        per_device,
        mesh=mesh,
        in_specs=(P("cls", "sy", "sx"), P(None, "cls", "sy", "sx"), P("sy", "sx")) + (P(),) * 6,
        out_specs=(P("cls", "sy", "sx"), P(None, "cls", "sy", "sx")),
        check_vma=False,
    )
```

```python
import functools

import jax
import jax.numpy as jnp
from jax import lax
from jax.experimental import pallas as pl
from jax.experimental.pallas import tpu as pltpu
from jax.sharding import PartitionSpec as P

MESH = pl.DeviceIdType.MESH
F32 = jnp.float32
BF16 = jnp.bfloat16
HIGH = lax.Precision.HIGHEST

SUB = 8
NEXT, OWN, REC, PREV, FAR = 0, 128, 256, 272, 400
ROWS_W = 528
HALO = 16
SIDE = 128


def dot_t(a, b):
    return lax.dot_general(a, b, (((1,), (1,)), ((), ())), precision=HIGH, preferred_element_type=F32)


def dot_h(a, b):
    return jnp.dot(a, b, precision=HIGH, preferred_element_type=F32)


def iota(shape, dim):
    return lax.broadcasted_iota(jnp.int32, shape, dim)


def split(x):
    hi = x.astype(BF16)
    return hi, (x - hi.astype(F32)).astype(BF16)


def kernel(
    a_hbm, st_hbm, hab_hbm, growth_hbm, surv_hbm, fec_hbm, rec_hbm, wr_hbm, wc_hbm,
    adj_out, sens_out,
    own, st_raw, hab, growth, surv, fec, rec, wr, wc, st, gath, wh, wl, xh, xl, rs_all, tabs, c1_all, d_all, c1_snd, d_snd, planes, mid, seed0, sp1, sp0,
    lsem, send, recv,
):
    ncls = 4
    p = lax.axis_index("cls")
    sy, sx = lax.axis_index("sy"), lax.axis_index("sx")
    nsy, nsx = lax.axis_size("sy"), lax.axis_size("sx")
    right, left = lax.rem(p + 1, ncls), lax.rem(p + ncls - 1, ncls)
    below, above = lax.rem(sy + 1, nsy), lax.rem(sy + nsy - 1, nsy)
    east, west = lax.rem(sx + 1, nsx), lax.rem(sx + nsx - 1, nsx)
    classes, rows, cols = own.shape
    quarter = rows // ncls
    inner = pl.ds(SIDE, cols)

    loads = [
        pltpu.make_async_copy(src, dst, lsem.at[k])
        for k, (src, dst) in enumerate(
            (
                (growth_hbm, growth), (surv_hbm, surv), (fec_hbm, fec), (rec_hbm, rec), (hab_hbm, hab),
                (a_hbm, own), (st_hbm, st_raw), (wr_hbm, wr), (wc_hbm, wc),
            )
        )
    ]
    barrier = pltpu.get_barrier_semaphore()
    for where in ({"cls": left}, {"cls": right}, {"sy": above}, {"sy": below}, {"sx": west}, {"sx": east}):
        pl.semaphore_signal(barrier, inc=1, device_id=where, device_id_type=MESH)
    for load in loads:
        load.start()

    def q_row(ahead, s):
        return pl.multiple_of(lax.rem(p + ahead, ncls) * quarter + s * SUB, SUB)

    def remote(src, dst, k, where):
        return pltpu.make_async_remote_copy(
            src_ref=src, dst_ref=dst, send_sem=send.at[k], recv_sem=recv.at[k], device_id=where, device_id_type=MESH
        )

    to_right, to_left = {"cls": right}, {"cls": left}
    piece = lambda ref, row: ref.at[:, pl.ds(row, SUB), :]
    far_r = [remote(piece(a_hbm, q_row(1, s)), gath.at[0, s, 1], 0 + s, to_right) for s in range(2)]
    far_l = [remote(piece(a_hbm, q_row(2, s)), gath.at[1, s, 0], 2 + s, to_left) for s in range(2)]
    near_r = [remote(piece(a_hbm, q_row(0, s)), gath.at[1, s, 1], 4 + s, to_right) for s in range(2)]
    near_l = [remote(piece(a_hbm, q_row(3, s)), gath.at[0, s, 0], 6 + s, to_left) for s in range(2)]
    fwd_r = [remote(gath.at[0, s, 1], gath.at[1, s, 2], 8 + s, to_right) for s in range(2)]
    fwd_l = [remote(gath.at[1, s, 0], gath.at[0, s, 2], 10 + s, to_left) for s in range(2)]
    half = classes // 2

    def returns(kind, s, k, first):
        at = pl.ds(first, half)
        dst = c1_all.at[at, pl.ds(q_row(3 * kind, s), SUB), :]
        return remote(c1_snd.at[kind, s, at], dst, k, (to_left, to_right)[kind])

    ret_c = [[returns(kind, s, 12 + 2 * kind + s, 0) for s in range(2)] for kind in range(2)]
    ret_c2 = [[returns(kind, s, 26 + 2 * kind + s, half) for s in range(2)] for kind in range(2)]
    ret_d = [
        [remote(d_snd.at[0, s], piece(d_all, q_row(0, s)), 16 + s, to_left) for s in range(2)],
        [remote(d_snd.at[1, s], piece(d_all, q_row(3, s)), 18 + s, to_right) for s in range(2)],
    ]

    def seed_part(ahead):
        return planes.at[pl.ds(0, 2), pl.ds(pl.multiple_of(HALO + q_row(ahead, 0), SUB), quarter), inner]

    seed_l = remote(seed_part(0), seed_part(0), 20, to_left)
    seed_r = remote(seed_part(3), seed_part(3), 21, to_right)
    halo_d = remote(
        planes.at[:, pl.ds(rows, HALO), inner], planes.at[:, pl.ds(0, HALO), inner], 22, {"sy": below}
    )
    halo_u = remote(
        planes.at[:, pl.ds(HALO, HALO), inner], planes.at[:, pl.ds(HALO + rows, HALO), inner], 23, {"sy": above}
    )
    halo_e = remote(planes.at[:, :, pl.ds(cols, SIDE)], planes.at[:, :, pl.ds(0, SIDE)], 24, {"sx": east})
    halo_w = remote(
        planes.at[:, :, pl.ds(SIDE, SIDE)], planes.at[:, :, pl.ds(SIDE + cols, SIDE)], 25, {"sx": west}
    )

    pl.semaphore_wait(barrier, 6)
    for s in range(2):
        far_r[s].start()
        far_l[s].start()
    for s in range(2):
        near_r[s].start()
        near_l[s].start()

    for load in loads:
        load.wait()

    def place_of(rel):
        return ((p + rel) & (ncls - 1)) * classes

    r = iota((ROWS_W, 64), 0)
    base = jnp.where(r < OWN, place_of(1), jnp.where(r < REC, place_of(0), jnp.where(r < FAR, place_of(3), place_of(2))))
    off = jnp.where(r < REC, r & 127, (r - PREV) & 127) >> 3
    is_rec = (r >= REC) & (r < PREV)
    pick = jnp.where((base + off == iota((ROWS_W, 64), 1)) & ~is_rec, 1.0, 0.0).astype(F32)
    g = growth[...]
    by_source = dot_t(pick, g) + jnp.where(is_rec, rec[...], 0.0)
    c = iota((512, 64), 0)
    place_c = jnp.where(c < 128, place_of(1), jnp.where(c < 256, place_of(0), jnp.where(c < 384, place_of(3), place_of(2))))
    pick_c = jnp.where(place_c + ((c & 127) >> 3) == iota((512, 64), 1), 1.0, 0.0).astype(F32)
    full = dot_t(by_source, pick_c)
    full = jnp.where((iota(full.shape, 0) & 7) == (iota(full.shape, 1) & 7), full, 0.0)
    w_hi, w_lo = split(full)
    wh[...] = w_hi
    wl[...] = w_lo

    level = jnp.where((iota((64, 8), 0) >> 3) == iota((64, 8), 1), 1.0, 0.0).astype(F32)

    def expand(table):
        wide = dot_t(table, level)
        return jnp.where((iota(wide.shape, 0) & 7) == (iota(wide.shape, 1) & 7), wide, 0.0)

    s_tab, f_tab = surv[...], fec[...]
    pick_own = pick[OWN:REC]
    k_surv = expand(dot_t(pick, s_tab))
    k_surv = jnp.concatenate([k_surv[:REC], k_surv[PREV:]], axis=0)
    gf_tab = dot_h(f_tab, g)
    rf_one = jnp.broadcast_to(rec[...], (8, 64))
    k_own = jnp.concatenate(
        [
            expand(dot_t(pick_own, s_tab)),
            expand(dot_t(pick_own, f_tab)),
            expand(dot_t(pick_own, gf_tab)),
            expand(dot_t(rf_one, f_tab)),
        ],
        axis=0,
    )

    def indicator(row):
        h = hab[pl.ds(row, SUB), :]
        return jnp.concatenate([jnp.where(h == k, 1.0, 0.0).astype(F32) for k in range(8)], axis=0)

    for kind in range(2):
        for s in range(2):
            rs_all[kind, s] = dot_h(k_surv, indicator(q_row(3 * kind, s)))

    def own_tables(t, carry):
        row = pl.multiple_of(t * SUB, SUB)
        res = dot_h(k_own, indicator(row))
        tabs[t] = res[:384]
        planes[2, pl.ds(pl.multiple_of(HALO + row, SUB), SUB), inner] = res[384:]
        return carry

    lax.fori_loop(0, rows // SUB, own_tables, 0)

    def widen(k, carry):
        st[0, k] = st_raw[0, k].astype(F32)
        st[1, k] = st_raw[1, k].astype(F32)
        return carry

    lax.fori_loop(0, classes, widen, 0)

    for s in range(2):
        far_r[s].wait_recv()
        fwd_r[s].start()
        far_l[s].wait_recv()
        fwd_l[s].start()

    def flat(x):
        return x.reshape(classes * SUB, cols)

    def product(lo, hi):
        a_hi, a_lo = xh[...], xl[...]
        w1, w2 = wh[lo:hi], wl[lo:hi]
        return (
            jnp.dot(w1, a_hi, preferred_element_type=F32)
            + jnp.dot(w1, a_lo, preferred_element_type=F32)
            + jnp.dot(w2, a_hi, preferred_element_type=F32)
        )

    def process(kind, s):
        row = q_row(3 * kind, s)
        prow = pl.multiple_of(HALO + row, SUB)
        blocks = (gath[kind, s, 0], own[:, pl.ds(row, SUB), :], gath[kind, s, 1], gath[kind, s, 2])
        for k, block in enumerate(blocks):
            xh[k * 128 : (k + 1) * 128], xl[k * 128 : (k + 1) * 128] = split(flat(block))
        res = product(0, ROWS_W)
        there = (res[PREV:FAR], res[NEXT:OWN])[kind]
        c1_snd[kind, s] = there.reshape(classes, SUB, cols)
        c1_all[:, pl.ds(row, SUB), :] = res[OWN:REC].reshape(classes, SUB, cols)
        planes[0, pl.ds(prow, SUB), inner] = res[REC : REC + SUB]
        for k, start in enumerate((NEXT, OWN, PREV, FAR)):
            xh[k * 128 : (k + 1) * 128], xl[k * 128 : (k + 1) * 128] = split(
                res[start : start + 128] * rs_all[kind, s, k * 128 : (k + 1) * 128]
            )
        if kind == 0:
            res = product(OWN, FAR)
            mine, seeds, there = res[:128], res[128:136], res[144:272]
        else:
            res = product(NEXT, PREV)
            there, mine, seeds = res[:128], res[128:256], res[256:264]
        d_snd[kind, s] = there.reshape(classes, SUB, cols)
        d_all[:, pl.ds(row, SUB), :] = mine.reshape(classes, SUB, cols)
        planes[1, pl.ds(prow, SUB), inner] = seeds

    def arrive(s):
        near_l[s].wait_recv()
        fwd_l[s].wait_recv()
        near_r[s].wait_recv()
        fwd_r[s].wait_recv()

    arrive(0)
    for kind in range(2):
        process(kind, 0)
        ret_c[kind][0].start()
    arrive(1)
    for kind in range(2):
        process(kind, 1)
    seed_l.start()
    seed_r.start()
    for kind in range(2):
        ret_c2[kind][0].start()

    seed_l.wait_recv()
    seed_r.wait_recv()
    halo_d.start()
    halo_u.start()
    for kind in range(2):
        ret_d[kind][0].start()
    for kind in range(2):
        ret_c[kind][1].start()
        ret_c2[kind][1].start()
    for kind in range(2):
        ret_d[kind][1].start()
    halo_d.wait_recv()
    halo_u.wait_recv()
    halo_e.start()
    halo_w.start()
    halo_e.wait_recv()
    halo_w.wait_recv()
    halo_d.wait_send()
    halo_u.wait_send()
    halo_e.wait_send()
    halo_w.wait_send()

    def inside(shape, first):
        y = iota(shape, 0) + (first - HALO) + sy * rows
        x = iota(shape, 1) - SIDE + sx * cols
        return (y >= 0) & (y < nsy * rows) & (x >= 0) & (x < nsx * cols)

    wide = cols + 2 * SIDE
    taps = wr.shape[0]
    reach = taps // 2

    def along_rows(load, row):
        total = wr[0] * load(row - reach)
        for k in range(1, taps):
            total = total + wr[k] * load(row - reach + k)
        return total

    def along_cols(x):
        total = wc[reach] * x
        for k in range(taps):
            if k != reach:
                total = total + wc[k] * pltpu.roll(x, (reach - k) % wide, axis=1)
        return total

    n_pad = rows + 2 * HALO

    for t in range(n_pad // SUB):
        at = pl.ds(t * SUB, SUB)
        mid[at, :] = jnp.where(inside((SUB, wide), t * SUB), planes[0, at, :], 0.0)
    for t in range(1, n_pad // SUB - 1):
        at = pl.ds(t * SUB, SUB)
        spread = along_cols(along_rows(lambda first: mid[pl.ds(first, SUB), :], t * SUB))
        if 2 <= t < 2 + rows // SUB:
            sp1[pl.ds((t - 2) * SUB, SUB), :] = spread[:, SIDE : SIDE + cols]
        seed0[at, :] = jnp.where(
            inside((SUB, wide), t * SUB), planes[1, at, :] + planes[2, at, :] * spread, 0.0
        )
    for t in range(2, 2 + rows // SUB):
        spread = along_cols(along_rows(lambda first: seed0[pl.ds(first, SUB), :], t * SUB))
        sp0[pl.ds((t - 2) * SUB, SUB), :] = spread[:, SIDE : SIDE + cols]

    def finish_c(row):
        at = pl.ds(row, SUB)
        sens_out[1, :, at, :] = st[1, :, at, :] * c1_all[:, at, :]

    def finish_d(row):
        at = pl.ds(row, SUB)
        t = row // SUB
        cube = lambda k: tabs[t, k * 128 : (k + 1) * 128].reshape(classes, SUB, cols)
        carried = d_all[:, at, :] + cube(2) * sp1[at, :][None]
        sens_out[0, :, at, :] = st[0, :, at, :] * carried
        adj_out[:, at, :] = cube(0) * carried + cube(1) * sp0[at, :][None]

    for kind in range(2):
        for s in range(2):
            finish_c(q_row(3 * kind, s))
            finish_d(q_row(3 * kind, s))
    for s in range(2):
        for kind in range(2):
            ret_c[kind][s].wait_recv()
            ret_c2[kind][s].wait_recv()
            finish_c(q_row(1 + kind, s))
        for kind in range(2):
            ret_d[kind][s].wait_recv()
            finish_d(q_row(1 + kind, s))
    for group in (far_r, far_l, near_r, near_l, fwd_r, fwd_l, *ret_c, *ret_c2, *ret_d, [seed_l, seed_r]):
        for copy in group:
            copy.wait_send()


def per_device(
    adjoint_final, stored_states, habitat, growth, survival, fecundity, recruit, disp_rows, disp_cols
):
    years, classes, rows, cols = stored_states.shape
    wide = cols + 2 * SIDE
    block = (classes, rows, cols)
    vmem = pl.BlockSpec(memory_space=pltpu.VMEM)
    hbm = pl.BlockSpec(memory_space=pltpu.HBM)
    packs = (2, 2, classes, SUB, cols)
    return pl.pallas_call(
        kernel,
        out_shape=(jax.ShapeDtypeStruct(block, F32), jax.ShapeDtypeStruct((years,) + block, F32)),
        in_specs=[hbm] * 9,
        out_specs=(vmem, vmem),
        scratch_shapes=[
            pltpu.VMEM(block, F32),
            pltpu.VMEM((years,) + block, BF16),
            pltpu.VMEM(habitat.shape, jnp.int32),
            pltpu.VMEM(growth.shape, F32),
            pltpu.VMEM(survival.shape, F32),
            pltpu.VMEM(fecundity.shape, F32),
            pltpu.VMEM((1,) + recruit.shape, F32),
            pltpu.SMEM(disp_rows.shape, F32),
            pltpu.SMEM(disp_cols.shape, F32),
            pltpu.VMEM((years,) + block, F32),
            pltpu.VMEM((2, 2, 3, classes, SUB, cols), F32),
            pltpu.VMEM((ROWS_W, 512), BF16),
            pltpu.VMEM((ROWS_W, 512), BF16),
            pltpu.VMEM((512, cols), BF16),
            pltpu.VMEM((512, cols), BF16),
            pltpu.VMEM((2, 2, 512, cols), F32),
            pltpu.VMEM((rows // SUB, 384, cols), F32),
            pltpu.VMEM(block, F32),
            pltpu.VMEM(block, F32),
            pltpu.VMEM(packs, F32),
            pltpu.VMEM(packs, F32),
            pltpu.VMEM((3, rows + 2 * HALO, wide), F32),
            pltpu.VMEM((rows + 2 * HALO, wide), F32),
            pltpu.VMEM((rows + 2 * HALO, wide), F32),
            pltpu.VMEM((rows, cols), F32),
            pltpu.VMEM((rows, cols), F32),
            pltpu.SemaphoreType.DMA((9,)),
            pltpu.SemaphoreType.DMA((30,)),
            pltpu.SemaphoreType.DMA((30,)),
        ],
        compiler_params=pltpu.CompilerParams(
            collective_id=0, has_side_effects=True, vmem_limit_bytes=32 << 20
        ),
        cost_estimate=pl.CostEstimate(flops=4 * 10**9, bytes_accessed=8 * 10**6, transcendentals=0),
    )(
        *(
            pltpu.with_memory_space_constraint(x, pltpu.HBM)
            for x in (
                adjoint_final, stored_states, habitat, growth, survival, fecundity, recruit.reshape(1, -1),
                disp_rows, disp_cols,
            )
        )
    )


def solution(mesh):
    return jax.shard_map(
        per_device,
        mesh=mesh,
        in_specs=(P("cls", "sy", "sx"), P(None, "cls", "sy", "sx"), P("sy", "sx")) + (P(),) * 6,
        out_specs=(P("cls", "sy", "sx"), P(None, "cls", "sy", "sx")),
        check_vma=False,
    )
```

```python
import functools

import jax
import jax.numpy as jnp
from jax import lax
from jax.experimental import pallas as pl
from jax.experimental.pallas import tpu as pltpu
from jax.sharding import PartitionSpec as P

MESH = pl.DeviceIdType.MESH
F32 = jnp.float32
BF16 = jnp.bfloat16
HIGH = lax.Precision.HIGHEST

SUB = 8
NEXT, OWN, REC, PREV, FAR = 0, 128, 256, 272, 400
ROWS_W = 528
HALO = 16
SIDE = 128


def dot_t(a, b):
    return lax.dot_general(a, b, (((1,), (1,)), ((), ())), precision=HIGH, preferred_element_type=F32)


def dot_h(a, b):
    return jnp.dot(a, b, precision=HIGH, preferred_element_type=F32)


def iota(shape, dim):
    return lax.broadcasted_iota(jnp.int32, shape, dim)


def split(x):
    hi = x.astype(BF16)
    return hi, (x - hi.astype(F32)).astype(BF16)


def kernel(
    a_hbm, st_hbm, hab_hbm, growth_hbm, surv_hbm, fec_hbm, rec_hbm, wr_hbm, wc_hbm,
    adj_out, sens_out,
    own, st_raw, hab, growth, surv, fec, rec, wr, wc, st, gath, wh, wl, xh, xl, rs_all, tabs, c1_all, d_all, c1_snd, d_snd, planes, mid, seed0, sp1, sp0,
    lsem, send, recv,
):
    ncls = 4
    p = lax.axis_index("cls")
    sy, sx = lax.axis_index("sy"), lax.axis_index("sx")
    nsy, nsx = lax.axis_size("sy"), lax.axis_size("sx")
    right, left = lax.rem(p + 1, ncls), lax.rem(p + ncls - 1, ncls)
    below, above = lax.rem(sy + 1, nsy), lax.rem(sy + nsy - 1, nsy)
    east, west = lax.rem(sx + 1, nsx), lax.rem(sx + nsx - 1, nsx)
    classes, rows, cols = own.shape
    quarter = rows // ncls
    inner = pl.ds(SIDE, cols)

    loads = [
        pltpu.make_async_copy(src, dst, lsem.at[k])
        for k, (src, dst) in enumerate(
            (
                (growth_hbm, growth), (surv_hbm, surv), (fec_hbm, fec), (rec_hbm, rec), (hab_hbm, hab),
                (a_hbm, own), (st_hbm, st_raw), (wr_hbm, wr), (wc_hbm, wc),
            )
        )
    ]
    barrier = pltpu.get_barrier_semaphore()
    for where in ({"cls": left}, {"cls": right}, {"sy": above}, {"sy": below}, {"sx": west}, {"sx": east}):
        pl.semaphore_signal(barrier, inc=1, device_id=where, device_id_type=MESH)
    for load in loads:
        load.start()

    def q_row(ahead, s):
        return pl.multiple_of(lax.rem(p + ahead, ncls) * quarter + s * SUB, SUB)

    def remote(src, dst, k, where):
        return pltpu.make_async_remote_copy(
            src_ref=src, dst_ref=dst, send_sem=send.at[k], recv_sem=recv.at[k], device_id=where, device_id_type=MESH
        )

    to_right, to_left = {"cls": right}, {"cls": left}
    piece = lambda ref, row: ref.at[:, pl.ds(row, SUB), :]
    far_r = [remote(piece(a_hbm, q_row(1, s)), gath.at[0, s, 1], 0 + s, to_right) for s in range(2)]
    far_l = [remote(piece(a_hbm, q_row(2, s)), gath.at[1, s, 0], 2 + s, to_left) for s in range(2)]
    near_r = [remote(piece(a_hbm, q_row(0, s)), gath.at[1, s, 1], 4 + s, to_right) for s in range(2)]
    near_l = [remote(piece(a_hbm, q_row(3, s)), gath.at[0, s, 0], 6 + s, to_left) for s in range(2)]
    fwd_r = [remote(gath.at[0, s, 1], gath.at[1, s, 2], 8 + s, to_right) for s in range(2)]
    fwd_l = [remote(gath.at[1, s, 0], gath.at[0, s, 2], 10 + s, to_left) for s in range(2)]
    ret_c = [
        [remote(c1_snd.at[0, s], piece(c1_all, q_row(0, s)), 12 + s, to_left) for s in range(2)],
        [remote(c1_snd.at[1, s], piece(c1_all, q_row(3, s)), 14 + s, to_right) for s in range(2)],
    ]
    ret_d = [
        [remote(d_snd.at[0, s], piece(d_all, q_row(0, s)), 16 + s, to_left) for s in range(2)],
        [remote(d_snd.at[1, s], piece(d_all, q_row(3, s)), 18 + s, to_right) for s in range(2)],
    ]

    def seed_part(ahead):
        return planes.at[pl.ds(0, 2), pl.ds(pl.multiple_of(HALO + q_row(ahead, 0), SUB), quarter), inner]

    seed_l = remote(seed_part(0), seed_part(0), 20, to_left)
    seed_r = remote(seed_part(3), seed_part(3), 21, to_right)
    halo_d = remote(
        planes.at[:, pl.ds(rows, HALO), inner], planes.at[:, pl.ds(0, HALO), inner], 22, {"sy": below}
    )
    halo_u = remote(
        planes.at[:, pl.ds(HALO, HALO), inner], planes.at[:, pl.ds(HALO + rows, HALO), inner], 23, {"sy": above}
    )
    halo_e = remote(planes.at[:, :, pl.ds(cols, SIDE)], planes.at[:, :, pl.ds(0, SIDE)], 24, {"sx": east})
    halo_w = remote(
        planes.at[:, :, pl.ds(SIDE, SIDE)], planes.at[:, :, pl.ds(SIDE + cols, SIDE)], 25, {"sx": west}
    )

    pl.semaphore_wait(barrier, 6)
    for s in range(2):
        far_r[s].start()
        far_l[s].start()
    for s in range(2):
        near_r[s].start()
        near_l[s].start()

    for load in loads:
        load.wait()

    def place_of(rel):
        return ((p + rel) & (ncls - 1)) * classes

    r = iota((ROWS_W, 64), 0)
    base = jnp.where(r < OWN, place_of(1), jnp.where(r < REC, place_of(0), jnp.where(r < FAR, place_of(3), place_of(2))))
    off = jnp.where(r < REC, r & 127, (r - PREV) & 127) >> 3
    is_rec = (r >= REC) & (r < PREV)
    pick = jnp.where((base + off == iota((ROWS_W, 64), 1)) & ~is_rec, 1.0, 0.0).astype(F32)
    g = growth[...]
    by_source = dot_t(pick, g) + jnp.where(is_rec, rec[...], 0.0)
    c = iota((512, 64), 0)
    place_c = jnp.where(c < 128, place_of(1), jnp.where(c < 256, place_of(0), jnp.where(c < 384, place_of(3), place_of(2))))
    pick_c = jnp.where(place_c + ((c & 127) >> 3) == iota((512, 64), 1), 1.0, 0.0).astype(F32)
    full = dot_t(by_source, pick_c)
    full = jnp.where((iota(full.shape, 0) & 7) == (iota(full.shape, 1) & 7), full, 0.0)
    w_hi, w_lo = split(full)
    wh[...] = w_hi
    wl[...] = w_lo

    level = jnp.where((iota((64, 8), 0) >> 3) == iota((64, 8), 1), 1.0, 0.0).astype(F32)

    def expand(table):
        wide = dot_t(table, level)
        return jnp.where((iota(wide.shape, 0) & 7) == (iota(wide.shape, 1) & 7), wide, 0.0)

    s_tab, f_tab = surv[...], fec[...]
    pick_own = pick[OWN:REC]
    k_surv = expand(dot_t(pick, s_tab))
    k_surv = jnp.concatenate([k_surv[:REC], k_surv[PREV:]], axis=0)
    gf_tab = dot_h(f_tab, g)
    rf_one = jnp.broadcast_to(rec[...], (8, 64))
    k_own = jnp.concatenate(
        [
            expand(dot_t(pick_own, s_tab)),
            expand(dot_t(pick_own, f_tab)),
            expand(dot_t(pick_own, gf_tab)),
            expand(dot_t(rf_one, f_tab)),
        ],
        axis=0,
    )

    def indicator(row):
        h = hab[pl.ds(row, SUB), :]
        return jnp.concatenate([jnp.where(h == k, 1.0, 0.0).astype(F32) for k in range(8)], axis=0)

    for kind in range(2):
        for s in range(2):
            rs_all[kind, s] = dot_h(k_surv, indicator(q_row(3 * kind, s)))

    def own_tables(t, carry):
        row = pl.multiple_of(t * SUB, SUB)
        res = dot_h(k_own, indicator(row))
        tabs[t] = res[:384]
        planes[2, pl.ds(pl.multiple_of(HALO + row, SUB), SUB), inner] = res[384:]
        return carry

    lax.fori_loop(0, rows // SUB, own_tables, 0)

    def widen(k, carry):
        st[0, k] = st_raw[0, k].astype(F32)
        st[1, k] = st_raw[1, k].astype(F32)
        return carry

    lax.fori_loop(0, classes, widen, 0)

    for s in range(2):
        far_r[s].wait_recv()
        fwd_r[s].start()
        far_l[s].wait_recv()
        fwd_l[s].start()

    def flat(x):
        return x.reshape(classes * SUB, cols)

    def product(lo, hi):
        a_hi, a_lo = xh[...], xl[...]
        w1, w2 = wh[lo:hi], wl[lo:hi]
        return (
            jnp.dot(w1, a_hi, preferred_element_type=F32)
            + jnp.dot(w1, a_lo, preferred_element_type=F32)
            + jnp.dot(w2, a_hi, preferred_element_type=F32)
        )

    def process(kind, s):
        row = q_row(3 * kind, s)
        prow = pl.multiple_of(HALO + row, SUB)
        blocks = (gath[kind, s, 0], own[:, pl.ds(row, SUB), :], gath[kind, s, 1], gath[kind, s, 2])
        for k, block in enumerate(blocks):
            xh[k * 128 : (k + 1) * 128], xl[k * 128 : (k + 1) * 128] = split(flat(block))
        res = product(0, ROWS_W)
        there = (res[PREV:FAR], res[NEXT:OWN])[kind]
        c1_snd[kind, s] = there.reshape(classes, SUB, cols)
        c1_all[:, pl.ds(row, SUB), :] = res[OWN:REC].reshape(classes, SUB, cols)
        planes[0, pl.ds(prow, SUB), inner] = res[REC : REC + SUB]
        for k, start in enumerate((NEXT, OWN, PREV, FAR)):
            xh[k * 128 : (k + 1) * 128], xl[k * 128 : (k + 1) * 128] = split(
                res[start : start + 128] * rs_all[kind, s, k * 128 : (k + 1) * 128]
            )
        if kind == 0:
            res = product(OWN, FAR)
            mine, seeds, there = res[:128], res[128:136], res[144:272]
        else:
            res = product(NEXT, PREV)
            there, mine, seeds = res[:128], res[128:256], res[256:264]
        d_snd[kind, s] = there.reshape(classes, SUB, cols)
        d_all[:, pl.ds(row, SUB), :] = mine.reshape(classes, SUB, cols)
        planes[1, pl.ds(prow, SUB), inner] = seeds

    def arrive(s):
        near_l[s].wait_recv()
        fwd_l[s].wait_recv()
        near_r[s].wait_recv()
        fwd_r[s].wait_recv()

    arrive(0)
    for kind in range(2):
        process(kind, 0)
        ret_c[kind][0].start()
    arrive(1)
    for kind in range(2):
        process(kind, 1)
    seed_l.start()
    seed_r.start()
    for kind in range(2):
        ret_d[kind][0].start()

    seed_l.wait_recv()
    seed_r.wait_recv()
    halo_d.start()
    halo_u.start()
    for kind in range(2):
        ret_c[kind][1].start()
    for kind in range(2):
        ret_d[kind][1].start()
    halo_d.wait_recv()
    halo_u.wait_recv()
    halo_e.start()
    halo_w.start()
    halo_e.wait_recv()
    halo_w.wait_recv()
    halo_d.wait_send()
    halo_u.wait_send()
    halo_e.wait_send()
    halo_w.wait_send()

    def inside(shape, first):
        y = iota(shape, 0) + (first - HALO) + sy * rows
        x = iota(shape, 1) - SIDE + sx * cols
        return (y >= 0) & (y < nsy * rows) & (x >= 0) & (x < nsx * cols)

    wide = cols + 2 * SIDE
    taps = wr.shape[0]
    reach = taps // 2

    def along_rows(load, row):
        total = wr[0] * load(row - reach)
        for k in range(1, taps):
            total = total + wr[k] * load(row - reach + k)
        return total

    def along_cols(x):
        total = wc[reach] * x
        for k in range(taps):
            if k != reach:
                total = total + wc[k] * pltpu.roll(x, (reach - k) % wide, axis=1)
        return total

    n_pad = rows + 2 * HALO

    for t in range(n_pad // SUB):
        at = pl.ds(t * SUB, SUB)
        mid[at, :] = jnp.where(inside((SUB, wide), t * SUB), planes[0, at, :], 0.0)
    for t in range(1, n_pad // SUB - 1):
        at = pl.ds(t * SUB, SUB)
        spread = along_cols(along_rows(lambda first: mid[pl.ds(first, SUB), :], t * SUB))
        if 2 <= t < 2 + rows // SUB:
            sp1[pl.ds((t - 2) * SUB, SUB), :] = spread[:, SIDE : SIDE + cols]
        seed0[at, :] = jnp.where(
            inside((SUB, wide), t * SUB), planes[1, at, :] + planes[2, at, :] * spread, 0.0
        )
    for t in range(2, 2 + rows // SUB):
        spread = along_cols(along_rows(lambda first: seed0[pl.ds(first, SUB), :], t * SUB))
        sp0[pl.ds((t - 2) * SUB, SUB), :] = spread[:, SIDE : SIDE + cols]

    def finish_c(row):
        at = pl.ds(row, SUB)
        sens_out[1, :, at, :] = st[1, :, at, :] * c1_all[:, at, :]

    def finish_d(row):
        at = pl.ds(row, SUB)
        t = row // SUB
        cube = lambda k: tabs[t, k * 128 : (k + 1) * 128].reshape(classes, SUB, cols)
        carried = d_all[:, at, :] + cube(2) * sp1[at, :][None]
        sens_out[0, :, at, :] = st[0, :, at, :] * carried
        adj_out[:, at, :] = cube(0) * carried + cube(1) * sp0[at, :][None]

    for kind in range(2):
        for s in range(2):
            finish_c(q_row(3 * kind, s))
            finish_d(q_row(3 * kind, s))
    for s in range(2):
        for kind in range(2):
            ret_c[kind][s].wait_recv()
            finish_c(q_row(1 + kind, s))
        for kind in range(2):
            ret_d[kind][s].wait_recv()
            finish_d(q_row(1 + kind, s))
    for group in (far_r, far_l, near_r, near_l, fwd_r, fwd_l, *ret_c, *ret_d, [seed_l, seed_r]):
        for copy in group:
            copy.wait_send()


def store(adj_in, sens_in, adj_out, sens_out, sem):
    classes = adj_in.shape[0]
    step = classes // 4
    copies = []
    for k in range(4):
        at = pl.ds(k * step, step)
        for src, dst in ((adj_in, adj_out), (sens_in.at[0], sens_out.at[0]), (sens_in.at[1], sens_out.at[1])):
            copies.append(pltpu.make_async_copy(src.at[at], dst.at[at], sem.at[len(copies)]))
    for copy in copies:
        copy.start()
    for copy in copies:
        copy.wait()


def per_device(
    adjoint_final, stored_states, habitat, growth, survival, fecundity, recruit, disp_rows, disp_cols
):
    years, classes, rows, cols = stored_states.shape
    wide = cols + 2 * SIDE
    block = (classes, rows, cols)
    vmem = pl.BlockSpec(memory_space=pltpu.VMEM)
    hbm = pl.BlockSpec(memory_space=pltpu.HBM)
    packs = (2, 2, classes, SUB, cols)
    shapes = (jax.ShapeDtypeStruct(block, F32), jax.ShapeDtypeStruct((years,) + block, F32))
    results = pl.pallas_call(
        kernel,
        out_shape=shapes,
        in_specs=[hbm] * 9,
        out_specs=(vmem, vmem),
        scratch_shapes=[
            pltpu.VMEM(block, F32),
            pltpu.VMEM((years,) + block, BF16),
            pltpu.VMEM(habitat.shape, jnp.int32),
            pltpu.VMEM(growth.shape, F32),
            pltpu.VMEM(survival.shape, F32),
            pltpu.VMEM(fecundity.shape, F32),
            pltpu.VMEM((1,) + recruit.shape, F32),
            pltpu.SMEM(disp_rows.shape, F32),
            pltpu.SMEM(disp_cols.shape, F32),
            pltpu.VMEM((years,) + block, F32),
            pltpu.VMEM((2, 2, 3, classes, SUB, cols), F32),
            pltpu.VMEM((ROWS_W, 512), BF16),
            pltpu.VMEM((ROWS_W, 512), BF16),
            pltpu.VMEM((512, cols), BF16),
            pltpu.VMEM((512, cols), BF16),
            pltpu.VMEM((2, 2, 512, cols), F32),
            pltpu.VMEM((rows // SUB, 384, cols), F32),
            pltpu.VMEM(block, F32),
            pltpu.VMEM(block, F32),
            pltpu.VMEM(packs, F32),
            pltpu.VMEM(packs, F32),
            pltpu.VMEM((3, rows + 2 * HALO, wide), F32),
            pltpu.VMEM((rows + 2 * HALO, wide), F32),
            pltpu.VMEM((rows + 2 * HALO, wide), F32),
            pltpu.VMEM((rows, cols), F32),
            pltpu.VMEM((rows, cols), F32),
            pltpu.SemaphoreType.DMA((9,)),
            pltpu.SemaphoreType.DMA((26,)),
            pltpu.SemaphoreType.DMA((26,)),
        ],
        compiler_params=pltpu.CompilerParams(
            collective_id=0, has_side_effects=True, vmem_limit_bytes=32 << 20
        ),
        cost_estimate=pl.CostEstimate(flops=4 * 10**9, bytes_accessed=8 * 10**6, transcendentals=0),
    )(
        *(
            pltpu.with_memory_space_constraint(x, pltpu.HBM)
            for x in (
                adjoint_final, stored_states, habitat, growth, survival, fecundity, recruit.reshape(1, -1),
                disp_rows, disp_cols,
            )
        )
    )
    return pl.pallas_call(
        store,
        out_shape=shapes,
        in_specs=[pl.BlockSpec(memory_space=pltpu.VMEM)] * 2,
        out_specs=(hbm, hbm),
        scratch_shapes=[pltpu.SemaphoreType.DMA((12,))],
        compiler_params=pltpu.CompilerParams(vmem_limit_bytes=1 << 20),
    )(*(pltpu.with_memory_space_constraint(x, pltpu.VMEM) for x in results))


def solution(mesh):
    return jax.shard_map(
        per_device,
        mesh=mesh,
        in_specs=(P("cls", "sy", "sx"), P(None, "cls", "sy", "sx"), P("sy", "sx")) + (P(),) * 6,
        out_specs=(P("cls", "sy", "sx"), P(None, "cls", "sy", "sx")),
        check_vma=False,
    )
```

```python
import functools

import jax
import jax.numpy as jnp
from jax import lax
from jax.experimental import pallas as pl
from jax.experimental.pallas import tpu as pltpu
from jax.sharding import PartitionSpec as P

MESH = pl.DeviceIdType.MESH
F32 = jnp.float32
BF16 = jnp.bfloat16
HIGH = lax.Precision.HIGHEST

SUB = 8
NEXT, OWN, REC, PREV, FAR = 0, 128, 256, 272, 400
ROWS_W = 528
HALO = 16
SIDE = 128


def dot_t(a, b):
    return lax.dot_general(a, b, (((1,), (1,)), ((), ())), precision=HIGH, preferred_element_type=F32)


def dot_h(a, b):
    return jnp.dot(a, b, precision=HIGH, preferred_element_type=F32)


def iota(shape, dim):
    return lax.broadcasted_iota(jnp.int32, shape, dim)


def split(x):
    hi = x.astype(BF16)
    return hi, (x - hi.astype(F32)).astype(BF16)


def kernel(
    a_hbm, st_hbm, hab_hbm, growth_hbm, surv_hbm, fec_hbm, rec_hbm, wr_hbm, wc_hbm,
    adj_out, sens_out,
    own, st_raw, hab, growth, surv, fec, rec, wr, wc, st, gath, wh, wl, xh, xl, rs_all, tabs, c1_all, d_all, c1_snd, d_snd, planes, mid, seed0, sp1, sp0,
    lsem, send, recv,
):
    ncls = 4
    p = lax.axis_index("cls")
    sy, sx = lax.axis_index("sy"), lax.axis_index("sx")
    nsy, nsx = lax.axis_size("sy"), lax.axis_size("sx")
    right, left = lax.rem(p + 1, ncls), lax.rem(p + ncls - 1, ncls)
    below, above = lax.rem(sy + 1, nsy), lax.rem(sy + nsy - 1, nsy)
    east, west = lax.rem(sx + 1, nsx), lax.rem(sx + nsx - 1, nsx)
    classes, rows, cols = own.shape
    quarter = rows // ncls
    inner = pl.ds(SIDE, cols)

    loads = [
        pltpu.make_async_copy(src, dst, lsem.at[k])
        for k, (src, dst) in enumerate(
            (
                (growth_hbm, growth), (surv_hbm, surv), (fec_hbm, fec), (rec_hbm, rec), (hab_hbm, hab),
                (a_hbm, own), (st_hbm, st_raw), (wr_hbm, wr), (wc_hbm, wc),
            )
        )
    ]
    barrier = pltpu.get_barrier_semaphore()
    for where in ({"cls": left}, {"cls": right}, {"sy": above}, {"sy": below}, {"sx": west}, {"sx": east}):
        pl.semaphore_signal(barrier, inc=1, device_id=where, device_id_type=MESH)
    for load in loads:
        load.start()

    def q_row(ahead, s):
        return pl.multiple_of(lax.rem(p + ahead, ncls) * quarter + s * SUB, SUB)

    def remote(src, dst, k, where):
        return pltpu.make_async_remote_copy(
            src_ref=src, dst_ref=dst, send_sem=send.at[k], recv_sem=recv.at[k], device_id=where, device_id_type=MESH
        )

    to_right, to_left = {"cls": right}, {"cls": left}
    piece = lambda ref, row: ref.at[:, pl.ds(row, SUB), :]
    far_r = [remote(piece(a_hbm, q_row(1, s)), gath.at[0, s, 1], 0 + s, to_right) for s in range(2)]
    far_l = [remote(piece(a_hbm, q_row(2, s)), gath.at[1, s, 0], 2 + s, to_left) for s in range(2)]
    near_r = [remote(piece(a_hbm, q_row(0, s)), gath.at[1, s, 1], 4 + s, to_right) for s in range(2)]
    near_l = [remote(piece(a_hbm, q_row(3, s)), gath.at[0, s, 0], 6 + s, to_left) for s in range(2)]
    fwd_r = [remote(gath.at[0, s, 1], gath.at[1, s, 2], 8 + s, to_right) for s in range(2)]
    fwd_l = [remote(gath.at[1, s, 0], gath.at[0, s, 2], 10 + s, to_left) for s in range(2)]
    ret_c = [
        [remote(c1_snd.at[0, s], piece(c1_all, q_row(0, s)), 12 + s, to_left) for s in range(2)],
        [remote(c1_snd.at[1, s], piece(c1_all, q_row(3, s)), 14 + s, to_right) for s in range(2)],
    ]
    ret_d = [
        [remote(d_snd.at[0, s], piece(d_all, q_row(0, s)), 16 + s, to_left) for s in range(2)],
        [remote(d_snd.at[1, s], piece(d_all, q_row(3, s)), 18 + s, to_right) for s in range(2)],
    ]

    def seed_part(ahead):
        return planes.at[pl.ds(0, 2), pl.ds(pl.multiple_of(HALO + q_row(ahead, 0), SUB), quarter), inner]

    seed_l = remote(seed_part(0), seed_part(0), 20, to_left)
    seed_r = remote(seed_part(3), seed_part(3), 21, to_right)
    halo_d = remote(
        planes.at[:, pl.ds(rows, HALO), inner], planes.at[:, pl.ds(0, HALO), inner], 22, {"sy": below}
    )
    halo_u = remote(
        planes.at[:, pl.ds(HALO, HALO), inner], planes.at[:, pl.ds(HALO + rows, HALO), inner], 23, {"sy": above}
    )
    halo_e = remote(planes.at[:, :, pl.ds(cols, SIDE)], planes.at[:, :, pl.ds(0, SIDE)], 24, {"sx": east})
    halo_w = remote(
        planes.at[:, :, pl.ds(SIDE, SIDE)], planes.at[:, :, pl.ds(SIDE + cols, SIDE)], 25, {"sx": west}
    )

    pl.semaphore_wait(barrier, 6)
    for first, second in ((far_r[0], far_l[0]), (near_r[0], near_l[0]), (far_r[1], far_l[1])):
        first.start()
        second.start()

    for load in loads:
        load.wait()

    def place_of(rel):
        return ((p + rel) & (ncls - 1)) * classes

    r = iota((ROWS_W, 64), 0)
    base = jnp.where(r < OWN, place_of(1), jnp.where(r < REC, place_of(0), jnp.where(r < FAR, place_of(3), place_of(2))))
    off = jnp.where(r < REC, r & 127, (r - PREV) & 127) >> 3
    is_rec = (r >= REC) & (r < PREV)
    pick = jnp.where((base + off == iota((ROWS_W, 64), 1)) & ~is_rec, 1.0, 0.0).astype(F32)
    g = growth[...]
    by_source = dot_t(pick, g) + jnp.where(is_rec, rec[...], 0.0)
    c = iota((512, 64), 0)
    place_c = jnp.where(c < 128, place_of(1), jnp.where(c < 256, place_of(0), jnp.where(c < 384, place_of(3), place_of(2))))
    pick_c = jnp.where(place_c + ((c & 127) >> 3) == iota((512, 64), 1), 1.0, 0.0).astype(F32)
    full = dot_t(by_source, pick_c)
    full = jnp.where((iota(full.shape, 0) & 7) == (iota(full.shape, 1) & 7), full, 0.0)
    w_hi, w_lo = split(full)
    wh[...] = w_hi
    wl[...] = w_lo

    far_r[0].wait_recv()
    fwd_r[0].start()
    far_l[0].wait_recv()
    fwd_l[0].start()
    near_r[1].start()
    near_l[1].start()

    level = jnp.where((iota((64, 8), 0) >> 3) == iota((64, 8), 1), 1.0, 0.0).astype(F32)

    def expand(table):
        wide = dot_t(table, level)
        return jnp.where((iota(wide.shape, 0) & 7) == (iota(wide.shape, 1) & 7), wide, 0.0)

    s_tab, f_tab = surv[...], fec[...]
    pick_own = pick[OWN:REC]
    k_surv = expand(dot_t(pick, s_tab))
    k_surv = jnp.concatenate([k_surv[:REC], k_surv[PREV:]], axis=0)
    gf_tab = dot_h(f_tab, g)
    rf_one = jnp.broadcast_to(rec[...], (8, 64))
    k_own = jnp.concatenate(
        [
            expand(dot_t(pick_own, s_tab)),
            expand(dot_t(pick_own, f_tab)),
            expand(dot_t(pick_own, gf_tab)),
            expand(dot_t(rf_one, f_tab)),
        ],
        axis=0,
    )

    def indicator(row):
        h = hab[pl.ds(row, SUB), :]
        return jnp.concatenate([jnp.where(h == k, 1.0, 0.0).astype(F32) for k in range(8)], axis=0)

    for kind in range(2):
        for s in range(2):
            rs_all[kind, s] = dot_h(k_surv, indicator(q_row(3 * kind, s)))

    def own_tables(t, carry):
        row = pl.multiple_of(t * SUB, SUB)
        res = dot_h(k_own, indicator(row))
        tabs[t] = res[:384]
        planes[2, pl.ds(pl.multiple_of(HALO + row, SUB), SUB), inner] = res[384:]
        return carry

    lax.fori_loop(0, rows // SUB, own_tables, 0)

    def widen(k, carry):
        st[0, k] = st_raw[0, k].astype(F32)
        st[1, k] = st_raw[1, k].astype(F32)
        return carry

    lax.fori_loop(0, classes, widen, 0)

    far_r[1].wait_recv()
    fwd_r[1].start()
    far_l[1].wait_recv()
    fwd_l[1].start()

    def flat(x):
        return x.reshape(classes * SUB, cols)

    def product(lo, hi):
        a_hi, a_lo = xh[...], xl[...]
        w1, w2 = wh[lo:hi], wl[lo:hi]
        return (
            jnp.dot(w1, a_hi, preferred_element_type=F32)
            + jnp.dot(w1, a_lo, preferred_element_type=F32)
            + jnp.dot(w2, a_hi, preferred_element_type=F32)
        )

    def process(kind, s):
        row = q_row(3 * kind, s)
        prow = pl.multiple_of(HALO + row, SUB)
        blocks = (gath[kind, s, 0], own[:, pl.ds(row, SUB), :], gath[kind, s, 1], gath[kind, s, 2])
        for k, block in enumerate(blocks):
            xh[k * 128 : (k + 1) * 128], xl[k * 128 : (k + 1) * 128] = split(flat(block))
        res = product(0, ROWS_W)
        there = (res[PREV:FAR], res[NEXT:OWN])[kind]
        c1_snd[kind, s] = there.reshape(classes, SUB, cols)
        c1_all[:, pl.ds(row, SUB), :] = res[OWN:REC].reshape(classes, SUB, cols)
        planes[0, pl.ds(prow, SUB), inner] = res[REC : REC + SUB]
        for k, start in enumerate((NEXT, OWN, PREV, FAR)):
            xh[k * 128 : (k + 1) * 128], xl[k * 128 : (k + 1) * 128] = split(
                res[start : start + 128] * rs_all[kind, s, k * 128 : (k + 1) * 128]
            )
        if kind == 0:
            res = product(OWN, FAR)
            mine, seeds, there = res[:128], res[128:136], res[144:272]
        else:
            res = product(NEXT, PREV)
            there, mine, seeds = res[:128], res[128:256], res[256:264]
        d_snd[kind, s] = there.reshape(classes, SUB, cols)
        d_all[:, pl.ds(row, SUB), :] = mine.reshape(classes, SUB, cols)
        planes[1, pl.ds(prow, SUB), inner] = seeds

    def arrive(s):
        near_l[s].wait_recv()
        fwd_l[s].wait_recv()
        near_r[s].wait_recv()
        fwd_r[s].wait_recv()

    arrive(0)
    for kind in range(2):
        process(kind, 0)
        ret_c[kind][0].start()
    arrive(1)
    for kind in range(2):
        process(kind, 1)
    seed_l.start()
    seed_r.start()
    for kind in range(2):
        ret_d[kind][0].start()

    seed_l.wait_recv()
    seed_r.wait_recv()
    halo_d.start()
    halo_u.start()
    for kind in range(2):
        ret_d[kind][1].start()
    for kind in range(2):
        ret_c[kind][1].start()
    halo_d.wait_recv()
    halo_u.wait_recv()
    halo_e.start()
    halo_w.start()
    halo_e.wait_recv()
    halo_w.wait_recv()
    halo_d.wait_send()
    halo_u.wait_send()
    halo_e.wait_send()
    halo_w.wait_send()

    def inside(shape, first):
        y = iota(shape, 0) + (first - HALO) + sy * rows
        x = iota(shape, 1) - SIDE + sx * cols
        return (y >= 0) & (y < nsy * rows) & (x >= 0) & (x < nsx * cols)

    wide = cols + 2 * SIDE
    taps = wr.shape[0]
    reach = taps // 2

    def along_rows(load, row):
        total = wr[0] * load(row - reach)
        for k in range(1, taps):
            total = total + wr[k] * load(row - reach + k)
        return total

    def along_cols(x):
        total = wc[reach] * x
        for k in range(taps):
            if k != reach:
                total = total + wc[k] * pltpu.roll(x, (reach - k) % wide, axis=1)
        return total

    n_pad = rows + 2 * HALO

    for t in range(n_pad // SUB):
        at = pl.ds(t * SUB, SUB)
        mid[at, :] = jnp.where(inside((SUB, wide), t * SUB), planes[0, at, :], 0.0)
    for t in range(1, n_pad // SUB - 1):
        at = pl.ds(t * SUB, SUB)
        spread = along_cols(along_rows(lambda first: mid[pl.ds(first, SUB), :], t * SUB))
        if 2 <= t < 2 + rows // SUB:
            sp1[pl.ds((t - 2) * SUB, SUB), :] = spread[:, SIDE : SIDE + cols]
        seed0[at, :] = jnp.where(
            inside((SUB, wide), t * SUB), planes[1, at, :] + planes[2, at, :] * spread, 0.0
        )
    for t in range(2, 2 + rows // SUB):
        spread = along_cols(along_rows(lambda first: seed0[pl.ds(first, SUB), :], t * SUB))
        sp0[pl.ds((t - 2) * SUB, SUB), :] = spread[:, SIDE : SIDE + cols]

    def finish_c(row):
        at = pl.ds(row, SUB)
        sens_out[1, :, at, :] = st[1, :, at, :] * c1_all[:, at, :]

    def finish_d(row):
        at = pl.ds(row, SUB)
        t = row // SUB
        cube = lambda k: tabs[t, k * 128 : (k + 1) * 128].reshape(classes, SUB, cols)
        carried = d_all[:, at, :] + cube(2) * sp1[at, :][None]
        sens_out[0, :, at, :] = st[0, :, at, :] * carried
        adj_out[:, at, :] = cube(0) * carried + cube(1) * sp0[at, :][None]

    for kind in range(2):
        for s in range(2):
            finish_c(q_row(3 * kind, s))
            finish_d(q_row(3 * kind, s))
    for s in range(2):
        for copies, finish in ((ret_c, finish_c), (ret_d, finish_d))[:: 1 - 2 * s]:
            for kind in range(2):
                copies[kind][s].wait_recv()
                finish(q_row(1 + kind, s))
    for group in (far_r, far_l, near_r, near_l, fwd_r, fwd_l, *ret_c, *ret_d, [seed_l, seed_r]):
        for copy in group:
            copy.wait_send()


def store(adj_in, sens_in, adj_out, sens_out, sem):
    classes = adj_in.shape[0]
    step = classes // 1
    copies = []
    for k in range(1):
        at = pl.ds(k * step, step)
        for src, dst in ((adj_in, adj_out), (sens_in.at[0], sens_out.at[0]), (sens_in.at[1], sens_out.at[1])):
            copies.append(pltpu.make_async_copy(src.at[at], dst.at[at], sem.at[len(copies)]))
    for copy in copies:
        copy.start()
    for copy in copies:
        copy.wait()


def per_device(
    adjoint_final, stored_states, habitat, growth, survival, fecundity, recruit, disp_rows, disp_cols
):
    years, classes, rows, cols = stored_states.shape
    wide = cols + 2 * SIDE
    block = (classes, rows, cols)
    vmem = pl.BlockSpec(memory_space=pltpu.VMEM)
    hbm = pl.BlockSpec(memory_space=pltpu.HBM)
    packs = (2, 2, classes, SUB, cols)
    shapes = (jax.ShapeDtypeStruct(block, F32), jax.ShapeDtypeStruct((years,) + block, F32))
    results = pl.pallas_call(
        kernel,
        out_shape=shapes,
        in_specs=[hbm] * 9,
        out_specs=(vmem, vmem),
        scratch_shapes=[
            pltpu.VMEM(block, F32),
            pltpu.VMEM((years,) + block, BF16),
            pltpu.VMEM(habitat.shape, jnp.int32),
            pltpu.VMEM(growth.shape, F32),
            pltpu.VMEM(survival.shape, F32),
            pltpu.VMEM(fecundity.shape, F32),
            pltpu.VMEM((1,) + recruit.shape, F32),
            pltpu.SMEM(disp_rows.shape, F32),
            pltpu.SMEM(disp_cols.shape, F32),
            pltpu.VMEM((years,) + block, F32),
            pltpu.VMEM((2, 2, 3, classes, SUB, cols), F32),
            pltpu.VMEM((ROWS_W, 512), BF16),
            pltpu.VMEM((ROWS_W, 512), BF16),
            pltpu.VMEM((512, cols), BF16),
            pltpu.VMEM((512, cols), BF16),
            pltpu.VMEM((2, 2, 512, cols), F32),
            pltpu.VMEM((rows // SUB, 384, cols), F32),
            pltpu.VMEM(block, F32),
            pltpu.VMEM(block, F32),
            pltpu.VMEM(packs, F32),
            pltpu.VMEM(packs, F32),
            pltpu.VMEM((3, rows + 2 * HALO, wide), F32),
            pltpu.VMEM((rows + 2 * HALO, wide), F32),
            pltpu.VMEM((rows + 2 * HALO, wide), F32),
            pltpu.VMEM((rows, cols), F32),
            pltpu.VMEM((rows, cols), F32),
            pltpu.SemaphoreType.DMA((9,)),
            pltpu.SemaphoreType.DMA((26,)),
            pltpu.SemaphoreType.DMA((26,)),
        ],
        compiler_params=pltpu.CompilerParams(
            collective_id=0, has_side_effects=True, vmem_limit_bytes=32 << 20
        ),
        cost_estimate=pl.CostEstimate(flops=4 * 10**9, bytes_accessed=8 * 10**6, transcendentals=0),
    )(
        *(
            pltpu.with_memory_space_constraint(x, pltpu.HBM)
            for x in (
                adjoint_final, stored_states, habitat, growth, survival, fecundity, recruit.reshape(1, -1),
                disp_rows, disp_cols,
            )
        )
    )
    return pl.pallas_call(
        store,
        out_shape=shapes,
        in_specs=[pl.BlockSpec(memory_space=pltpu.VMEM)] * 2,
        out_specs=(hbm, hbm),
        scratch_shapes=[pltpu.SemaphoreType.DMA((3,))],
        compiler_params=pltpu.CompilerParams(vmem_limit_bytes=1 << 20),
    )(*(pltpu.with_memory_space_constraint(x, pltpu.VMEM) for x in results))


def solution(mesh):
    return jax.shard_map(
        per_device,
        mesh=mesh,
        in_specs=(P("cls", "sy", "sx"), P(None, "cls", "sy", "sx"), P("sy", "sx")) + (P(),) * 6,
        out_specs=(P("cls", "sy", "sx"), P(None, "cls", "sy", "sx")),
        check_vma=False,
    )
```

```python
import functools

import jax
import jax.numpy as jnp
from jax import lax
from jax.experimental import pallas as pl
from jax.experimental.pallas import tpu as pltpu
from jax.sharding import PartitionSpec as P

MESH = pl.DeviceIdType.MESH
F32 = jnp.float32
BF16 = jnp.bfloat16
HIGH = lax.Precision.HIGHEST

SUB = 8
NEXT, OWN, REC, PREV, FAR = 0, 128, 256, 272, 400
ROWS_W = 528
HALO = 16
SIDE = 128


def dot_t(a, b):
    return lax.dot_general(a, b, (((1,), (1,)), ((), ())), precision=HIGH, preferred_element_type=F32)


def dot_h(a, b):
    return jnp.dot(a, b, precision=HIGH, preferred_element_type=F32)


def iota(shape, dim):
    return lax.broadcasted_iota(jnp.int32, shape, dim)


def split(x):
    hi = x.astype(BF16)
    return hi, (x - hi.astype(F32)).astype(BF16)


def kernel(
    a_hbm, st_hbm, hab_hbm, growth_hbm, surv_hbm, fec_hbm, rec_hbm, wr_hbm, wc_hbm,
    adj_out, sens_out,
    own, st_raw, hab, growth, surv, fec, rec, wr, wc, st, gath, wh, wl, xh, xl, rs_all, tabs, c1_all, d_all, c1_snd, d_snd, planes, mid, seed0, sp1, sp0,
    lsem, send, recv,
):
    ncls = 4
    p = lax.axis_index("cls")
    sy, sx = lax.axis_index("sy"), lax.axis_index("sx")
    nsy, nsx = lax.axis_size("sy"), lax.axis_size("sx")
    right, left = lax.rem(p + 1, ncls), lax.rem(p + ncls - 1, ncls)
    below, above = lax.rem(sy + 1, nsy), lax.rem(sy + nsy - 1, nsy)
    east, west = lax.rem(sx + 1, nsx), lax.rem(sx + nsx - 1, nsx)
    classes, rows, cols = own.shape
    quarter = rows // ncls
    inner = pl.ds(SIDE, cols)

    loads = [
        pltpu.make_async_copy(src, dst, lsem.at[k])
        for k, (src, dst) in enumerate(
            (
                (growth_hbm, growth), (surv_hbm, surv), (fec_hbm, fec), (rec_hbm, rec), (hab_hbm, hab),
                (a_hbm, own), (st_hbm, st_raw), (wr_hbm, wr), (wc_hbm, wc),
            )
        )
    ]
    barrier = pltpu.get_barrier_semaphore()
    for where in ({"cls": left}, {"cls": right}, {"sy": above}, {"sy": below}, {"sx": west}, {"sx": east}):
        pl.semaphore_signal(barrier, inc=1, device_id=where, device_id_type=MESH)
    for load in loads:
        load.start()

    def q_row(ahead, s):
        return pl.multiple_of(lax.rem(p + ahead, ncls) * quarter + s * SUB, SUB)

    def remote(src, dst, k, where):
        return pltpu.make_async_remote_copy(
            src_ref=src, dst_ref=dst, send_sem=send.at[k], recv_sem=recv.at[k], device_id=where, device_id_type=MESH
        )

    to_right, to_left = {"cls": right}, {"cls": left}
    piece = lambda ref, row: ref.at[:, pl.ds(row, SUB), :]
    far_r = [remote(piece(a_hbm, q_row(1, s)), gath.at[0, s, 1], 0 + s, to_right) for s in range(2)]
    far_l = [remote(piece(a_hbm, q_row(2, s)), gath.at[1, s, 0], 2 + s, to_left) for s in range(2)]
    near_r = [remote(piece(a_hbm, q_row(0, s)), gath.at[1, s, 1], 4 + s, to_right) for s in range(2)]
    near_l = [remote(piece(a_hbm, q_row(3, s)), gath.at[0, s, 0], 6 + s, to_left) for s in range(2)]
    fwd_r = [remote(gath.at[0, s, 1], gath.at[1, s, 2], 8 + s, to_right) for s in range(2)]
    fwd_l = [remote(gath.at[1, s, 0], gath.at[0, s, 2], 10 + s, to_left) for s in range(2)]
    ret_c = [
        [remote(c1_snd.at[0, s], piece(c1_all, q_row(0, s)), 12 + s, to_left) for s in range(2)],
        [remote(c1_snd.at[1, s], piece(c1_all, q_row(3, s)), 14 + s, to_right) for s in range(2)],
    ]
    ret_d = [
        [remote(d_snd.at[0, s], piece(d_all, q_row(0, s)), 16 + s, to_left) for s in range(2)],
        [remote(d_snd.at[1, s], piece(d_all, q_row(3, s)), 18 + s, to_right) for s in range(2)],
    ]

    def seed_part(ahead):
        return planes.at[pl.ds(0, 2), pl.ds(pl.multiple_of(HALO + q_row(ahead, 0), SUB), quarter), inner]

    seed_l = remote(seed_part(0), seed_part(0), 20, to_left)
    seed_r = remote(seed_part(3), seed_part(3), 21, to_right)
    halo_d = remote(
        planes.at[:, pl.ds(rows, HALO), inner], planes.at[:, pl.ds(0, HALO), inner], 22, {"sy": below}
    )
    halo_u = remote(
        planes.at[:, pl.ds(HALO, HALO), inner], planes.at[:, pl.ds(HALO + rows, HALO), inner], 23, {"sy": above}
    )
    halo_e = remote(planes.at[:, :, pl.ds(cols, SIDE)], planes.at[:, :, pl.ds(0, SIDE)], 24, {"sx": east})
    halo_w = remote(
        planes.at[:, :, pl.ds(SIDE, SIDE)], planes.at[:, :, pl.ds(SIDE + cols, SIDE)], 25, {"sx": west}
    )

    pl.semaphore_wait(barrier, 6)
    for first, second in ((far_r[0], far_l[0]), (far_r[1], far_l[1])):
        first.start()
        second.start()

    for load in loads:
        load.wait()

    def place_of(rel):
        return ((p + rel) & (ncls - 1)) * classes

    r = iota((ROWS_W, 64), 0)
    base = jnp.where(r < OWN, place_of(1), jnp.where(r < REC, place_of(0), jnp.where(r < FAR, place_of(3), place_of(2))))
    off = jnp.where(r < REC, r & 127, (r - PREV) & 127) >> 3
    is_rec = (r >= REC) & (r < PREV)
    pick = jnp.where((base + off == iota((ROWS_W, 64), 1)) & ~is_rec, 1.0, 0.0).astype(F32)
    g = growth[...]
    by_source = dot_t(pick, g) + jnp.where(is_rec, rec[...], 0.0)
    c = iota((512, 64), 0)
    place_c = jnp.where(c < 128, place_of(1), jnp.where(c < 256, place_of(0), jnp.where(c < 384, place_of(3), place_of(2))))
    pick_c = jnp.where(place_c + ((c & 127) >> 3) == iota((512, 64), 1), 1.0, 0.0).astype(F32)
    full = dot_t(by_source, pick_c)
    full = jnp.where((iota(full.shape, 0) & 7) == (iota(full.shape, 1) & 7), full, 0.0)
    w_hi, w_lo = split(full)
    wh[...] = w_hi
    wl[...] = w_lo

    far_r[0].wait_recv()
    fwd_r[0].start()
    far_l[0].wait_recv()
    fwd_l[0].start()
    near_r[0].start()
    near_l[0].start()

    level = jnp.where((iota((64, 8), 0) >> 3) == iota((64, 8), 1), 1.0, 0.0).astype(F32)

    def expand(table):
        wide = dot_t(table, level)
        return jnp.where((iota(wide.shape, 0) & 7) == (iota(wide.shape, 1) & 7), wide, 0.0)

    s_tab, f_tab = surv[...], fec[...]
    pick_own = pick[OWN:REC]
    k_surv = expand(dot_t(pick, s_tab))
    k_surv = jnp.concatenate([k_surv[:REC], k_surv[PREV:]], axis=0)
    gf_tab = dot_h(f_tab, g)
    rf_one = jnp.broadcast_to(rec[...], (8, 64))
    k_own = jnp.concatenate(
        [
            expand(dot_t(pick_own, s_tab)),
            expand(dot_t(pick_own, f_tab)),
            expand(dot_t(pick_own, gf_tab)),
            expand(dot_t(rf_one, f_tab)),
        ],
        axis=0,
    )

    def indicator(row):
        h = hab[pl.ds(row, SUB), :]
        return jnp.concatenate([jnp.where(h == k, 1.0, 0.0).astype(F32) for k in range(8)], axis=0)

    for kind in range(2):
        for s in range(2):
            rs_all[kind, s] = dot_h(k_surv, indicator(q_row(3 * kind, s)))

    far_r[1].wait_recv()
    fwd_r[1].start()
    far_l[1].wait_recv()
    fwd_l[1].start()
    near_r[1].start()
    near_l[1].start()

    def own_tables(t, carry):
        row = pl.multiple_of(t * SUB, SUB)
        res = dot_h(k_own, indicator(row))
        tabs[t] = res[:384]
        planes[2, pl.ds(pl.multiple_of(HALO + row, SUB), SUB), inner] = res[384:]
        return carry

    lax.fori_loop(0, rows // SUB, own_tables, 0)

    def widen(k, carry):
        st[0, k] = st_raw[0, k].astype(F32)
        st[1, k] = st_raw[1, k].astype(F32)
        return carry

    lax.fori_loop(0, classes, widen, 0)


    def flat(x):
        return x.reshape(classes * SUB, cols)

    def product(lo, hi):
        a_hi, a_lo = xh[...], xl[...]
        w1, w2 = wh[lo:hi], wl[lo:hi]
        return (
            jnp.dot(w1, a_hi, preferred_element_type=F32)
            + jnp.dot(w1, a_lo, preferred_element_type=F32)
            + jnp.dot(w2, a_hi, preferred_element_type=F32)
        )

    def process(kind, s):
        row = q_row(3 * kind, s)
        prow = pl.multiple_of(HALO + row, SUB)
        blocks = (gath[kind, s, 0], own[:, pl.ds(row, SUB), :], gath[kind, s, 1], gath[kind, s, 2])
        for k, block in enumerate(blocks):
            xh[k * 128 : (k + 1) * 128], xl[k * 128 : (k + 1) * 128] = split(flat(block))
        res = product(0, ROWS_W)
        there = (res[PREV:FAR], res[NEXT:OWN])[kind]
        c1_snd[kind, s] = there.reshape(classes, SUB, cols)
        c1_all[:, pl.ds(row, SUB), :] = res[OWN:REC].reshape(classes, SUB, cols)
        planes[0, pl.ds(prow, SUB), inner] = res[REC : REC + SUB]
        for k, start in enumerate((NEXT, OWN, PREV, FAR)):
            xh[k * 128 : (k + 1) * 128], xl[k * 128 : (k + 1) * 128] = split(
                res[start : start + 128] * rs_all[kind, s, k * 128 : (k + 1) * 128]
            )
        if kind == 0:
            res = product(OWN, FAR)
            mine, seeds, there = res[:128], res[128:136], res[144:272]
        else:
            res = product(NEXT, PREV)
            there, mine, seeds = res[:128], res[128:256], res[256:264]
        d_snd[kind, s] = there.reshape(classes, SUB, cols)
        d_all[:, pl.ds(row, SUB), :] = mine.reshape(classes, SUB, cols)
        planes[1, pl.ds(prow, SUB), inner] = seeds

    def arrive(s):
        near_l[s].wait_recv()
        fwd_l[s].wait_recv()
        near_r[s].wait_recv()
        fwd_r[s].wait_recv()

    arrive(0)
    for kind in range(2):
        process(kind, 0)
        ret_c[kind][0].start()
    arrive(1)
    for kind in range(2):
        process(kind, 1)
    seed_l.start()
    seed_r.start()
    for kind in range(2):
        ret_d[kind][0].start()

    seed_l.wait_recv()
    seed_r.wait_recv()
    halo_d.start()
    halo_u.start()
    for kind in range(2):
        ret_d[kind][1].start()
    for kind in range(2):
        ret_c[kind][1].start()
    halo_d.wait_recv()
    halo_u.wait_recv()
    halo_e.start()
    halo_w.start()
    halo_e.wait_recv()
    halo_w.wait_recv()
    halo_d.wait_send()
    halo_u.wait_send()
    halo_e.wait_send()
    halo_w.wait_send()

    def inside(shape, first):
        y = iota(shape, 0) + (first - HALO) + sy * rows
        x = iota(shape, 1) - SIDE + sx * cols
        return (y >= 0) & (y < nsy * rows) & (x >= 0) & (x < nsx * cols)

    wide = cols + 2 * SIDE
    taps = wr.shape[0]
    reach = taps // 2

    def along_rows(load, row):
        total = wr[0] * load(row - reach)
        for k in range(1, taps):
            total = total + wr[k] * load(row - reach + k)
        return total

    def along_cols(x):
        total = wc[reach] * x
        for k in range(taps):
            if k != reach:
                total = total + wc[k] * pltpu.roll(x, (reach - k) % wide, axis=1)
        return total

    n_pad = rows + 2 * HALO

    for t in range(n_pad // SUB):
        at = pl.ds(t * SUB, SUB)
        mid[at, :] = jnp.where(inside((SUB, wide), t * SUB), planes[0, at, :], 0.0)
    for t in range(1, n_pad // SUB - 1):
        at = pl.ds(t * SUB, SUB)
        spread = along_cols(along_rows(lambda first: mid[pl.ds(first, SUB), :], t * SUB))
        if 2 <= t < 2 + rows // SUB:
            sp1[pl.ds((t - 2) * SUB, SUB), :] = spread[:, SIDE : SIDE + cols]
        seed0[at, :] = jnp.where(
            inside((SUB, wide), t * SUB), planes[1, at, :] + planes[2, at, :] * spread, 0.0
        )
    for t in range(2, 2 + rows // SUB):
        spread = along_cols(along_rows(lambda first: seed0[pl.ds(first, SUB), :], t * SUB))
        sp0[pl.ds((t - 2) * SUB, SUB), :] = spread[:, SIDE : SIDE + cols]

    def finish_c(row):
        at = pl.ds(row, SUB)
        sens_out[1, :, at, :] = st[1, :, at, :] * c1_all[:, at, :]

    def finish_d(row):
        at = pl.ds(row, SUB)
        t = row // SUB
        cube = lambda k: tabs[t, k * 128 : (k + 1) * 128].reshape(classes, SUB, cols)
        carried = d_all[:, at, :] + cube(2) * sp1[at, :][None]
        sens_out[0, :, at, :] = st[0, :, at, :] * carried
        adj_out[:, at, :] = cube(0) * carried + cube(1) * sp0[at, :][None]

    for kind in range(2):
        for s in range(2):
            finish_c(q_row(3 * kind, s))
            finish_d(q_row(3 * kind, s))
    for s in range(2):
        for copies, finish in ((ret_c, finish_c), (ret_d, finish_d))[:: 1 - 2 * s]:
            for kind in range(2):
                copies[kind][s].wait_recv()
                finish(q_row(1 + kind, s))
    for group in (far_r, far_l, near_r, near_l, fwd_r, fwd_l, *ret_c, *ret_d, [seed_l, seed_r]):
        for copy in group:
            copy.wait_send()


def store(adj_in, sens_in, adj_out, sens_out, sem):
    classes = adj_in.shape[0]
    step = classes // 1
    copies = []
    for k in range(1):
        at = pl.ds(k * step, step)
        for src, dst in ((adj_in, adj_out), (sens_in.at[0], sens_out.at[0]), (sens_in.at[1], sens_out.at[1])):
            copies.append(pltpu.make_async_copy(src.at[at], dst.at[at], sem.at[len(copies)]))
    for copy in copies:
        copy.start()
    for copy in copies:
        copy.wait()


def per_device(
    adjoint_final, stored_states, habitat, growth, survival, fecundity, recruit, disp_rows, disp_cols
):
    years, classes, rows, cols = stored_states.shape
    wide = cols + 2 * SIDE
    block = (classes, rows, cols)
    vmem = pl.BlockSpec(memory_space=pltpu.VMEM)
    hbm = pl.BlockSpec(memory_space=pltpu.HBM)
    packs = (2, 2, classes, SUB, cols)
    shapes = (jax.ShapeDtypeStruct(block, F32), jax.ShapeDtypeStruct((years,) + block, F32))
    results = pl.pallas_call(
        kernel,
        out_shape=shapes,
        in_specs=[hbm] * 9,
        out_specs=(vmem, vmem),
        scratch_shapes=[
            pltpu.VMEM(block, F32),
            pltpu.VMEM((years,) + block, BF16),
            pltpu.VMEM(habitat.shape, jnp.int32),
            pltpu.VMEM(growth.shape, F32),
            pltpu.VMEM(survival.shape, F32),
            pltpu.VMEM(fecundity.shape, F32),
            pltpu.VMEM((1,) + recruit.shape, F32),
            pltpu.SMEM(disp_rows.shape, F32),
            pltpu.SMEM(disp_cols.shape, F32),
            pltpu.VMEM((years,) + block, F32),
            pltpu.VMEM((2, 2, 3, classes, SUB, cols), F32),
            pltpu.VMEM((ROWS_W, 512), BF16),
            pltpu.VMEM((ROWS_W, 512), BF16),
            pltpu.VMEM((512, cols), BF16),
            pltpu.VMEM((512, cols), BF16),
            pltpu.VMEM((2, 2, 512, cols), F32),
            pltpu.VMEM((rows // SUB, 384, cols), F32),
            pltpu.VMEM(block, F32),
            pltpu.VMEM(block, F32),
            pltpu.VMEM(packs, F32),
            pltpu.VMEM(packs, F32),
            pltpu.VMEM((3, rows + 2 * HALO, wide), F32),
            pltpu.VMEM((rows + 2 * HALO, wide), F32),
            pltpu.VMEM((rows + 2 * HALO, wide), F32),
            pltpu.VMEM((rows, cols), F32),
            pltpu.VMEM((rows, cols), F32),
            pltpu.SemaphoreType.DMA((9,)),
            pltpu.SemaphoreType.DMA((26,)),
            pltpu.SemaphoreType.DMA((26,)),
        ],
        compiler_params=pltpu.CompilerParams(
            collective_id=0, has_side_effects=True, vmem_limit_bytes=32 << 20
        ),
        cost_estimate=pl.CostEstimate(flops=4 * 10**9, bytes_accessed=8 * 10**6, transcendentals=0),
    )(
        *(
            pltpu.with_memory_space_constraint(x, pltpu.HBM)
            for x in (
                adjoint_final, stored_states, habitat, growth, survival, fecundity, recruit.reshape(1, -1),
                disp_rows, disp_cols,
            )
        )
    )
    return pl.pallas_call(
        store,
        out_shape=shapes,
        in_specs=[pl.BlockSpec(memory_space=pltpu.VMEM)] * 2,
        out_specs=(hbm, hbm),
        scratch_shapes=[pltpu.SemaphoreType.DMA((3,))],
        compiler_params=pltpu.CompilerParams(vmem_limit_bytes=1 << 20),
    )(*(pltpu.with_memory_space_constraint(x, pltpu.VMEM) for x in results))


def solution(mesh):
    return jax.shard_map(
        per_device,
        mesh=mesh,
        in_specs=(P("cls", "sy", "sx"), P(None, "cls", "sy", "sx"), P("sy", "sx")) + (P(),) * 6,
        out_specs=(P("cls", "sy", "sx"), P(None, "cls", "sy", "sx")),
        check_vma=False,
    )
```

```python
import functools

import jax
import jax.numpy as jnp
from jax import lax
from jax.experimental import pallas as pl
from jax.experimental.pallas import tpu as pltpu
from jax.sharding import PartitionSpec as P

MESH = pl.DeviceIdType.MESH
F32 = jnp.float32
BF16 = jnp.bfloat16
HIGH = lax.Precision.HIGHEST

SUB = 8
NEXT, OWN, REC, PREV, FAR = 0, 128, 256, 272, 400
ROWS_W = 528
HALO = 16
SIDE = 128


def dot_t(a, b):
    return lax.dot_general(a, b, (((1,), (1,)), ((), ())), precision=HIGH, preferred_element_type=F32)


def dot_h(a, b):
    return jnp.dot(a, b, precision=HIGH, preferred_element_type=F32)


def iota(shape, dim):
    return lax.broadcasted_iota(jnp.int32, shape, dim)


def split(x):
    hi = x.astype(BF16)
    return hi, (x - hi.astype(F32)).astype(BF16)


def kernel(
    a_hbm, st_hbm, hab_hbm, growth_hbm, surv_hbm, fec_hbm, rec_hbm, wr_hbm, wc_hbm,
    adj_out, sens_out,
    own, st_raw, hab, growth, surv, fec, rec, wr, wc, st, gath, wh, wl, xh, xl, rs_all, tabs, c1_all, d_all, c1_snd, d_snd, planes, mid, seed0, sp1, sp0,
    lsem, send, recv,
):
    ncls = 4
    p = lax.axis_index("cls")
    sy, sx = lax.axis_index("sy"), lax.axis_index("sx")
    nsy, nsx = lax.axis_size("sy"), lax.axis_size("sx")
    right, left = lax.rem(p + 1, ncls), lax.rem(p + ncls - 1, ncls)
    below, above = lax.rem(sy + 1, nsy), lax.rem(sy + nsy - 1, nsy)
    east, west = lax.rem(sx + 1, nsx), lax.rem(sx + nsx - 1, nsx)
    classes, rows, cols = own.shape
    quarter = rows // ncls
    inner = pl.ds(SIDE, cols)

    loads = [
        pltpu.make_async_copy(src, dst, lsem.at[k])
        for k, (src, dst) in enumerate(
            (
                (growth_hbm, growth), (surv_hbm, surv), (fec_hbm, fec), (rec_hbm, rec), (hab_hbm, hab),
                (a_hbm, own), (st_hbm, st_raw), (wr_hbm, wr), (wc_hbm, wc),
            )
        )
    ]
    barrier = pltpu.get_barrier_semaphore()
    for where in ({"cls": left}, {"cls": right}, {"sy": above}, {"sy": below}, {"sx": west}, {"sx": east}):
        pl.semaphore_signal(barrier, inc=1, device_id=where, device_id_type=MESH)
    for load in loads:
        load.start()

    def q_row(ahead, s):
        return pl.multiple_of(lax.rem(p + ahead, ncls) * quarter + s * SUB, SUB)

    def remote(src, dst, k, where):
        return pltpu.make_async_remote_copy(
            src_ref=src, dst_ref=dst, send_sem=send.at[k], recv_sem=recv.at[k], device_id=where, device_id_type=MESH
        )

    to_right, to_left = {"cls": right}, {"cls": left}
    piece = lambda ref, row: ref.at[:, pl.ds(row, SUB), :]
    far_r = [remote(piece(a_hbm, q_row(1, s)), gath.at[0, s, 1], 0 + s, to_right) for s in range(2)]
    far_l = [remote(piece(a_hbm, q_row(2, s)), gath.at[1, s, 0], 2 + s, to_left) for s in range(2)]
    near_r = [remote(piece(a_hbm, q_row(0, s)), gath.at[1, s, 1], 4 + s, to_right) for s in range(2)]
    near_l = [remote(piece(a_hbm, q_row(3, s)), gath.at[0, s, 0], 6 + s, to_left) for s in range(2)]
    fwd_r = [remote(gath.at[0, s, 1], gath.at[1, s, 2], 8 + s, to_right) for s in range(2)]
    fwd_l = [remote(gath.at[1, s, 0], gath.at[0, s, 2], 10 + s, to_left) for s in range(2)]
    ret_c = [
        [remote(c1_snd.at[0, s], piece(c1_all, q_row(0, s)), 12 + s, to_left) for s in range(2)],
        [remote(c1_snd.at[1, s], piece(c1_all, q_row(3, s)), 14 + s, to_right) for s in range(2)],
    ]
    ret_d = [
        [remote(d_snd.at[0, s], piece(d_all, q_row(0, s)), 16 + s, to_left) for s in range(2)],
        [remote(d_snd.at[1, s], piece(d_all, q_row(3, s)), 18 + s, to_right) for s in range(2)],
    ]

    def seed_part(ahead):
        return planes.at[pl.ds(0, 2), pl.ds(pl.multiple_of(HALO + q_row(ahead, 0), SUB), quarter), inner]

    seed_l = remote(seed_part(0), seed_part(0), 20, to_left)
    seed_r = remote(seed_part(3), seed_part(3), 21, to_right)
    def halo_rows(up, k):
        made = []
        for n, (which, deep) in enumerate(((pl.ds(0, 1), HALO), (pl.ds(1, 2), SUB))):
            src = HALO if up else HALO + rows - deep
            dst = HALO + rows if up else HALO - deep
            made.append(
                remote(
                    planes.at[which, pl.ds(src, deep), inner], planes.at[which, pl.ds(dst, deep), inner],
                    k + n, {"sy": above if up else below},
                )
            )
        return made

    def halo_cols(back, k):
        made = []
        for n, (which, first) in enumerate(((pl.ds(0, 1), 0), (pl.ds(1, 2), SUB))):
            at = pl.ds(first, rows + 2 * (HALO - first))
            src, dst = (SIDE, SIDE + cols) if back else (cols, 0)
            made.append(
                remote(
                    planes.at[which, at, pl.ds(src, SIDE)], planes.at[which, at, pl.ds(dst, SIDE)],
                    k + n, {"sx": west if back else east},
                )
            )
        return made

    row_halos = halo_rows(False, 22) + halo_rows(True, 24)
    col_halos = halo_cols(False, 26) + halo_cols(True, 28)

    pl.semaphore_wait(barrier, 6)
    for first, second in ((far_r[0], far_l[0]), (near_r[0], near_l[0]), (far_r[1], far_l[1])):
        first.start()
        second.start()

    for load in loads:
        load.wait()

    def place_of(rel):
        return ((p + rel) & (ncls - 1)) * classes

    r = iota((ROWS_W, 64), 0)
    base = jnp.where(r < OWN, place_of(1), jnp.where(r < REC, place_of(0), jnp.where(r < FAR, place_of(3), place_of(2))))
    off = jnp.where(r < REC, r & 127, (r - PREV) & 127) >> 3
    is_rec = (r >= REC) & (r < PREV)
    pick = jnp.where((base + off == iota((ROWS_W, 64), 1)) & ~is_rec, 1.0, 0.0).astype(F32)
    g = growth[...]
    by_source = dot_t(pick, g) + jnp.where(is_rec, rec[...], 0.0)
    c = iota((512, 64), 0)
    place_c = jnp.where(c < 128, place_of(1), jnp.where(c < 256, place_of(0), jnp.where(c < 384, place_of(3), place_of(2))))
    pick_c = jnp.where(place_c + ((c & 127) >> 3) == iota((512, 64), 1), 1.0, 0.0).astype(F32)
    full = dot_t(by_source, pick_c)
    full = jnp.where((iota(full.shape, 0) & 7) == (iota(full.shape, 1) & 7), full, 0.0)
    w_hi, w_lo = split(full)
    wh[...] = w_hi
    wl[...] = w_lo

    far_r[0].wait_recv()
    fwd_r[0].start()
    far_l[0].wait_recv()
    fwd_l[0].start()
    near_r[1].start()
    near_l[1].start()

    level = jnp.where((iota((64, 8), 0) >> 3) == iota((64, 8), 1), 1.0, 0.0).astype(F32)

    def expand(table):
        wide = dot_t(table, level)
        return jnp.where((iota(wide.shape, 0) & 7) == (iota(wide.shape, 1) & 7), wide, 0.0)

    s_tab, f_tab = surv[...], fec[...]
    pick_own = pick[OWN:REC]
    k_surv = expand(dot_t(pick, s_tab))
    k_surv = jnp.concatenate([k_surv[:REC], k_surv[PREV:]], axis=0)
    gf_tab = dot_h(f_tab, g)
    rf_one = jnp.broadcast_to(rec[...], (8, 64))
    k_own = jnp.concatenate(
        [
            expand(dot_t(pick_own, s_tab)),
            expand(dot_t(pick_own, f_tab)),
            expand(dot_t(pick_own, gf_tab)),
            expand(dot_t(rf_one, f_tab)),
        ],
        axis=0,
    )

    def indicator(row):
        h = hab[pl.ds(row, SUB), :]
        return jnp.concatenate([jnp.where(h == k, 1.0, 0.0).astype(F32) for k in range(8)], axis=0)

    for kind in range(2):
        for s in range(2):
            rs_all[kind, s] = dot_h(k_surv, indicator(q_row(3 * kind, s)))

    def own_tables(t, carry):
        row = pl.multiple_of(t * SUB, SUB)
        res = dot_h(k_own, indicator(row))
        tabs[t] = res[:384]
        planes[2, pl.ds(pl.multiple_of(HALO + row, SUB), SUB), inner] = res[384:]
        return carry

    lax.fori_loop(0, rows // SUB, own_tables, 0)

    def widen(k, carry):
        st[0, k] = st_raw[0, k].astype(F32)
        st[1, k] = st_raw[1, k].astype(F32)
        return carry

    lax.fori_loop(0, classes, widen, 0)

    far_r[1].wait_recv()
    fwd_r[1].start()
    far_l[1].wait_recv()
    fwd_l[1].start()

    def flat(x):
        return x.reshape(classes * SUB, cols)

    def product(lo, hi):
        a_hi, a_lo = xh[...], xl[...]
        w1, w2 = wh[lo:hi], wl[lo:hi]
        return (
            jnp.dot(w1, a_hi, preferred_element_type=F32)
            + jnp.dot(w1, a_lo, preferred_element_type=F32)
            + jnp.dot(w2, a_hi, preferred_element_type=F32)
        )

    def process(kind, s):
        row = q_row(3 * kind, s)
        prow = pl.multiple_of(HALO + row, SUB)
        blocks = (gath[kind, s, 0], own[:, pl.ds(row, SUB), :], gath[kind, s, 1], gath[kind, s, 2])
        for k, block in enumerate(blocks):
            xh[k * 128 : (k + 1) * 128], xl[k * 128 : (k + 1) * 128] = split(flat(block))
        res = product(0, ROWS_W)
        there = (res[PREV:FAR], res[NEXT:OWN])[kind]
        c1_snd[kind, s] = there.reshape(classes, SUB, cols)
        c1_all[:, pl.ds(row, SUB), :] = res[OWN:REC].reshape(classes, SUB, cols)
        planes[0, pl.ds(prow, SUB), inner] = res[REC : REC + SUB]
        for k, start in enumerate((NEXT, OWN, PREV, FAR)):
            xh[k * 128 : (k + 1) * 128], xl[k * 128 : (k + 1) * 128] = split(
                res[start : start + 128] * rs_all[kind, s, k * 128 : (k + 1) * 128]
            )
        if kind == 0:
            res = product(OWN, FAR)
            mine, seeds, there = res[:128], res[128:136], res[144:272]
        else:
            res = product(NEXT, PREV)
            there, mine, seeds = res[:128], res[128:256], res[256:264]
        d_snd[kind, s] = there.reshape(classes, SUB, cols)
        d_all[:, pl.ds(row, SUB), :] = mine.reshape(classes, SUB, cols)
        planes[1, pl.ds(prow, SUB), inner] = seeds

    def arrive(s):
        near_l[s].wait_recv()
        fwd_l[s].wait_recv()
        near_r[s].wait_recv()
        fwd_r[s].wait_recv()

    arrive(0)
    for kind in range(2):
        process(kind, 0)
        ret_c[kind][0].start()
    arrive(1)
    for kind in range(2):
        process(kind, 1)
    seed_l.start()
    seed_r.start()
    for kind in range(2):
        ret_d[kind][0].start()

    seed_l.wait_recv()
    seed_r.wait_recv()
    for copy in row_halos:
        copy.start()
    for kind in range(2):
        ret_d[kind][1].start()
    for kind in range(2):
        ret_c[kind][1].start()
    for copy in row_halos:
        copy.wait_recv()
    for copy in col_halos:
        copy.start()
    for copy in col_halos:
        copy.wait_recv()
    for copy in row_halos + col_halos:
        copy.wait_send()

    def inside(shape, first):
        y = iota(shape, 0) + (first - HALO) + sy * rows
        x = iota(shape, 1) - SIDE + sx * cols
        return (y >= 0) & (y < nsy * rows) & (x >= 0) & (x < nsx * cols)

    wide = cols + 2 * SIDE
    taps = wr.shape[0]
    reach = taps // 2

    def along_rows(load, row):
        total = wr[0] * load(row - reach)
        for k in range(1, taps):
            total = total + wr[k] * load(row - reach + k)
        return total

    def along_cols(x):
        total = wc[reach] * x
        for k in range(taps):
            if k != reach:
                total = total + wc[k] * pltpu.roll(x, (reach - k) % wide, axis=1)
        return total

    n_pad = rows + 2 * HALO

    for t in range(n_pad // SUB):
        at = pl.ds(t * SUB, SUB)
        mid[at, :] = jnp.where(inside((SUB, wide), t * SUB), planes[0, at, :], 0.0)
    for t in range(1, n_pad // SUB - 1):
        at = pl.ds(t * SUB, SUB)
        spread = along_cols(along_rows(lambda first: mid[pl.ds(first, SUB), :], t * SUB))
        if 2 <= t < 2 + rows // SUB:
            sp1[pl.ds((t - 2) * SUB, SUB), :] = spread[:, SIDE : SIDE + cols]
        seed0[at, :] = jnp.where(
            inside((SUB, wide), t * SUB), planes[1, at, :] + planes[2, at, :] * spread, 0.0
        )
    for t in range(2, 2 + rows // SUB):
        spread = along_cols(along_rows(lambda first: seed0[pl.ds(first, SUB), :], t * SUB))
        sp0[pl.ds((t - 2) * SUB, SUB), :] = spread[:, SIDE : SIDE + cols]

    def finish_c(row):
        at = pl.ds(row, SUB)
        sens_out[1, :, at, :] = st[1, :, at, :] * c1_all[:, at, :]

    def finish_d(row):
        at = pl.ds(row, SUB)
        t = row // SUB
        cube = lambda k: tabs[t, k * 128 : (k + 1) * 128].reshape(classes, SUB, cols)
        carried = d_all[:, at, :] + cube(2) * sp1[at, :][None]
        sens_out[0, :, at, :] = st[0, :, at, :] * carried
        adj_out[:, at, :] = cube(0) * carried + cube(1) * sp0[at, :][None]

    for kind in range(2):
        for s in range(2):
            finish_c(q_row(3 * kind, s))
            finish_d(q_row(3 * kind, s))
    for s in range(2):
        for copies, finish in ((ret_c, finish_c), (ret_d, finish_d))[:: 1 - 2 * s]:
            for kind in range(2):
                copies[kind][s].wait_recv()
                finish(q_row(1 + kind, s))
    for group in (far_r, far_l, near_r, near_l, fwd_r, fwd_l, *ret_c, *ret_d, [seed_l, seed_r]):
        for copy in group:
            copy.wait_send()


def store(adj_in, sens_in, adj_out, sens_out, sem):
    classes = adj_in.shape[0]
    step = classes // 1
    copies = []
    for k in range(1):
        at = pl.ds(k * step, step)
        for src, dst in ((adj_in, adj_out), (sens_in.at[0], sens_out.at[0]), (sens_in.at[1], sens_out.at[1])):
            copies.append(pltpu.make_async_copy(src.at[at], dst.at[at], sem.at[len(copies)]))
    for copy in copies:
        copy.start()
    for copy in copies:
        copy.wait()


def per_device(
    adjoint_final, stored_states, habitat, growth, survival, fecundity, recruit, disp_rows, disp_cols
):
    years, classes, rows, cols = stored_states.shape
    wide = cols + 2 * SIDE
    block = (classes, rows, cols)
    vmem = pl.BlockSpec(memory_space=pltpu.VMEM)
    hbm = pl.BlockSpec(memory_space=pltpu.HBM)
    packs = (2, 2, classes, SUB, cols)
    shapes = (jax.ShapeDtypeStruct(block, F32), jax.ShapeDtypeStruct((years,) + block, F32))
    results = pl.pallas_call(
        kernel,
        out_shape=shapes,
        in_specs=[hbm] * 9,
        out_specs=(vmem, vmem),
        scratch_shapes=[
            pltpu.VMEM(block, F32),
            pltpu.VMEM((years,) + block, BF16),
            pltpu.VMEM(habitat.shape, jnp.int32),
            pltpu.VMEM(growth.shape, F32),
            pltpu.VMEM(survival.shape, F32),
            pltpu.VMEM(fecundity.shape, F32),
            pltpu.VMEM((1,) + recruit.shape, F32),
            pltpu.SMEM(disp_rows.shape, F32),
            pltpu.SMEM(disp_cols.shape, F32),
            pltpu.VMEM((years,) + block, F32),
            pltpu.VMEM((2, 2, 3, classes, SUB, cols), F32),
            pltpu.VMEM((ROWS_W, 512), BF16),
            pltpu.VMEM((ROWS_W, 512), BF16),
            pltpu.VMEM((512, cols), BF16),
            pltpu.VMEM((512, cols), BF16),
            pltpu.VMEM((2, 2, 512, cols), F32),
            pltpu.VMEM((rows // SUB, 384, cols), F32),
            pltpu.VMEM(block, F32),
            pltpu.VMEM(block, F32),
            pltpu.VMEM(packs, F32),
            pltpu.VMEM(packs, F32),
            pltpu.VMEM((3, rows + 2 * HALO, wide), F32),
            pltpu.VMEM((rows + 2 * HALO, wide), F32),
            pltpu.VMEM((rows + 2 * HALO, wide), F32),
            pltpu.VMEM((rows, cols), F32),
            pltpu.VMEM((rows, cols), F32),
            pltpu.SemaphoreType.DMA((9,)),
            pltpu.SemaphoreType.DMA((30,)),
            pltpu.SemaphoreType.DMA((30,)),
        ],
        compiler_params=pltpu.CompilerParams(
            collective_id=0, has_side_effects=True, vmem_limit_bytes=32 << 20
        ),
        cost_estimate=pl.CostEstimate(flops=4 * 10**9, bytes_accessed=8 * 10**6, transcendentals=0),
    )(
        *(
            pltpu.with_memory_space_constraint(x, pltpu.HBM)
            for x in (
                adjoint_final, stored_states, habitat, growth, survival, fecundity, recruit.reshape(1, -1),
                disp_rows, disp_cols,
            )
        )
    )
    return pl.pallas_call(
        store,
        out_shape=shapes,
        in_specs=[pl.BlockSpec(memory_space=pltpu.VMEM)] * 2,
        out_specs=(hbm, hbm),
        scratch_shapes=[pltpu.SemaphoreType.DMA((3,))],
        compiler_params=pltpu.CompilerParams(vmem_limit_bytes=1 << 20),
    )(*(pltpu.with_memory_space_constraint(x, pltpu.VMEM) for x in results))


def solution(mesh):
    return jax.shard_map(
        per_device,
        mesh=mesh,
        in_specs=(P("cls", "sy", "sx"), P(None, "cls", "sy", "sx"), P("sy", "sx")) + (P(),) * 6,
        out_specs=(P("cls", "sy", "sx"), P(None, "cls", "sy", "sx")),
        check_vma=False,
    )
```
